256 devices in a mesh: gx: 32 (over y, z), gy: 4 (over x_lo, core), ma: 2 (over x_hi).
Axes of the slice: x: 4 (x_hi: 2, x_lo: 2; x = x_hi * 2 + x_lo), y: 4, z: 8, core: 2. Of those that a mesh axis runs over, the one named last changes fastest.
Arguments:
- x_modes: bfloat16 [64, 48, 128, 256], P('gx', 'gy', None, 'ma'), may hold values from -45 to 45
- p_dirs: bfloat16 [64, 48, 128, 256], P('gx', 'gy', None, 'ma'), may hold values from -45 to 45
- permittivity: float32 [64, 48, 128], P('gx', 'gy'), may hold values from 1 to 12
- ritz_values: float32 [256], P('ma'), may hold values from 0.05 to 1
- blocks: bfloat16 [16, 128, 128], replicated, may hold values from -0.25 to 0.25
- adj_types: int32 [5, 64, 48], P(None, 'gx', 'gy'), may hold values from 0 to 15
- x_link: int32 [2, 32, 48], P(None, 'gx', 'gy'), may hold values from 0 to 11
- coeffs: bfloat16 [3, 256, 256], replicated, may hold values from -0.21875 to 0.21875
Outputs:
- x_next: bfloat16 [64, 48, 128, 256], P('gx', 'gy', None, 'ma')
- gram_k: float32 [3, 256, 3, 256], P(None, None, None, 'ma')
- gram_m: float32 [3, 256, 3, 256], P(None, None, None, 'ma')
The draws below stay inside these ranges and needn't reach their ends.
Inputs may be any that keep to these rules, and one draw needn't show every extreme that they name: `x_link`: a row counted within its group of 12 rows.
All inputs are finite; a program needn't handle non-finite values.
Results may differ from the reference program's by a relative error of at most 0.0075.
Values may be sent and summed in bfloat16 or wider, within the bound.
A program may use at most 128 MiB of HBM per device.

```python
import math
import jax
import jax.numpy as jnp
from jax import lax

EDGE = 128
MODES = 256
NTYPES = 16
CPX = 2
CPY = 12
NPX = 64
NPY = 48
XBLOCKS = 32


def modal_draw(key):
    subkeys = jax.random.split(key, 5)
    shape = (NPX, NPY, EDGE, MODES)
    normal = jax.random.normal(subkeys[0], shape, jnp.float32)
    values = normal
    values = jnp.clip(values, -5.0, 5.0)
    position = (jnp.arange(NPX, dtype=jnp.float32) / NPX).reshape(NPX, 1, 1, 1)
    rough_part = jax.random.uniform(subkeys[3], (NPX, NPY, EDGE, 1), jnp.float32)
    row_scale = 0.3 * jnp.exp(math.log(10.0) * (0.5 * position + 0.5 * rough_part))
    col_scale = 0.3 * jnp.exp(math.log(10.0) * jax.random.uniform(subkeys[4], (MODES,), jnp.float32))
    return (values * row_scale * col_scale).astype(jnp.bfloat16)


def draw_x_modes(key, part):
    key = jax.random.fold_in(key, 11)
    return modal_draw(key)


def draw_p_dirs(key, part):
    key = jax.random.fold_in(key, 23)
    return modal_draw(key)


def touch_ends(result, rng, least, top_value):
    extent = result.shape
    place = [jax.random.randint(jax.random.fold_in(rng, axis), (), 0, extent[axis]) for axis in range(len(extent))]
    result = result.at[tuple(place)].set(least)
    longest = extent.index(max(extent))
    place[longest] = (place[longest] + 1) % extent[longest]
    return result.at[tuple(place)].set(top_value)


def block_scale(own_key, extent, cuts, low, largest):
    loudness = 1.0
    for dim, blocks in cuts:
        heights = jax.random.uniform(jax.random.fold_in(jax.random.fold_in(own_key, 6), dim), (blocks,), jnp.float32, low / len(cuts), largest / len(cuts))
        loudness = loudness * jnp.repeat(jnp.exp(heights), extent[dim] // blocks).reshape((-1,) + (1,) * (len(extent) - 1 - dim))
    return loudness


def bell_draw(key, shape, width, bound, held_as=jnp.bfloat16):
    entries = jax.random.normal(key, shape, jnp.float32) * width
    return jnp.minimum(jnp.maximum(entries, -bound), bound).astype(held_as)


def setup_inputs(seed: int = 0) -> dict:
    streams_of = jax.random.split(jax.random.key(seed), 9)
    x_modes = draw_x_modes(jax.random.fold_in(streams_of[8], 71), 0)
    p_dirs = draw_p_dirs(jax.random.fold_in(streams_of[8], 71), 0)
    permittivity = jnp.clip(jnp.exp(math.log(12.0) - 2.4849066 * jax.random.uniform(streams_of[2], (NPX, NPY, EDGE), jnp.float32) ** block_scale(streams_of[2], (NPX, NPY, EDGE), ((0, 32), (1, 4)), -0.2, 0.2)), 1.0, 12.0)
    ritz_values = jnp.clip(jnp.exp(math.log(1.0) - 2.9957323 * jax.random.uniform(streams_of[3], (MODES,), jnp.float32) ** block_scale(streams_of[3], (MODES,), ((0, 2),), -0.2, 0.2)), 0.05, 1.0)
    blocks = bell_draw(streams_of[4], (NTYPES, EDGE, EDGE), (5 * EDGE) ** -0.5, 0.25)
    adj_types = touch_ends(jax.random.randint(streams_of[5], (5, NPX, NPY), 0, NTYPES), jax.random.fold_in(streams_of[5], 1), 0, NTYPES - 1).astype(jnp.int32)
    x_link = touch_ends(jax.random.randint(streams_of[6], (2, XBLOCKS, NPY), 0, CPY), jax.random.fold_in(streams_of[6], 1), 0, CPY - 1).astype(jnp.int32)
    coeffs = bell_draw(streams_of[7], (3, MODES, MODES), (3 * MODES) ** -0.5, 0.21875)
    return dict(x_modes=x_modes, p_dirs=p_dirs, permittivity=permittivity, ritz_values=ritz_values, blocks=blocks, adj_types=adj_types, x_link=x_link, coeffs=coeffs)


def pick(array, index, axis):
    return lax.dynamic_index_in_dim(array, index, axis, keepdims=False)

def curl_column(fetch, column_id, blocks, adj_types, x_link):
    columns_total = adj_types.shape[1]
    rows_total = adj_types.shape[2]
    centre = fetch(column_id)
    lower_col = fetch((column_id - 1) % columns_total)
    upper_col = fetch((column_id + 1) % columns_total)
    row_ids = jnp.arange(rows_total, dtype=jnp.int32)
    row_base = row_ids // CPY * CPY
    group = (column_id // CPX).astype(jnp.int32)
    lower_ids = jnp.where(column_id % CPX == 0, row_base + pick(x_link[0], group, 0), row_ids).astype(jnp.int32)
    upper_ids = jnp.where(column_id % CPX == CPX - 1, row_base + pick(x_link[1], group, 0), row_ids).astype(jnp.int32)
    lower_col = jnp.take(lower_col, lower_ids, axis=0)
    upper_col = jnp.take(upper_col, upper_ids, axis=0)
    zero_row = jnp.zeros_like(centre[:1])
    below_row = jnp.concatenate([zero_row, centre[:-1]], axis=0)
    above_row = jnp.concatenate([centre[1:], zero_row], axis=0)
    neighbours = jnp.stack([centre, lower_col, upper_col, below_row, above_row]).astype(jnp.float32)
    tile_ids = pick(adj_types, column_id, 1)
    tile_set = blocks.astype(jnp.float32)[tile_ids]
    return jnp.einsum('syet,sytm->yem', tile_set, neighbours)

def reference(x_modes, p_dirs, permittivity, ritz_values, blocks, adj_types, x_link, coeffs):
    columns_total, rows_total, edge_count, mode_count = x_modes.shape
    edges_total = columns_total * rows_total * edge_count
    column_ids = jnp.arange(columns_total, dtype=jnp.int32)

    def fetch_both(column_id):
        return jnp.concatenate([pick(x_modes, column_id, 0), pick(p_dirs, column_id, 0)], axis=-1)

    def residual(column_id):
        image_xp = curl_column(fetch_both, column_id, blocks, adj_types, x_link)
        permit = pick(permittivity, column_id, 0)[..., None]
        resid = image_xp[..., :mode_count] - permit * pick(x_modes, column_id, 0).astype(jnp.float32) * ritz_values
        return (resid, image_xp, permit)

    def accumulate(norm_total, column_id):
        resid, image_xp, permit = residual(column_id)
        return (norm_total + lax.optimization_barrier(jnp.sum(permit * resid * resid, axis=(0, 1))), None)
    norm_total, unused = lax.scan(accumulate, jnp.zeros((mode_count,), jnp.float32), column_ids)
    inv_norm = lax.rsqrt(norm_total / edges_total + 1e-06)

    def scaled(column_id):
        return (residual(column_id)[0] * inv_norm).astype(jnp.bfloat16)
    w_modes = lax.map(scaled, column_ids)

    def fetch_w(column_id):
        return pick(w_modes, column_id, 0)
    coef = coeffs.astype(jnp.float32)

    def gram_step(carry, column_id):
        gram_k, gram_m = carry
        unused_r, image_xp, permit = residual(column_id)
        image_w = curl_column(fetch_w, column_id, blocks, adj_types, x_link)
        panels = jnp.stack([pick(x_modes, column_id, 0), fetch_w(column_id), pick(p_dirs, column_id, 0)])
        images = jnp.stack([image_xp[..., :mode_count], image_w, image_xp[..., mode_count:]]).astype(jnp.bfloat16)
        masses = (permit[None] * panels.astype(jnp.float32)).astype(jnp.bfloat16)
        flat_panels = panels.astype(jnp.float32).reshape(3, -1, mode_count)
        flat_images = images.astype(jnp.float32).reshape(3, -1, mode_count)
        flat_masses = masses.astype(jnp.float32).reshape(3, -1, mode_count)
        gram_k = gram_k + jnp.einsum('xem,yen->xmyn', flat_panels, flat_images)
        gram_m = gram_m + jnp.einsum('xem,yen->xmyn', flat_panels, flat_masses)
        x_next = jnp.einsum('xyem,xmn->yen', panels.astype(jnp.float32), coef).astype(jnp.bfloat16)
        return ((gram_k, gram_m), x_next)
    zeros = jnp.zeros((3, mode_count, 3, mode_count), jnp.float32)
    (gram_k, gram_m), x_next = lax.scan(gram_step, (zeros, zeros), column_ids)
    return (x_next, gram_k / edges_total, gram_m / edges_total)
```

```python
import functools
import jax
import jax.numpy as jnp
from jax import lax
from jax.experimental import pallas as pl
from jax.experimental.pallas import tpu as pltpu
from jax.sharding import PartitionSpec as P

MESH = pl.DeviceIdType.MESH
F32 = jnp.float32
BF16 = jnp.bfloat16
EDGE = 128
HALF = 128
COLS = 2
ROWS = 12
PATCHES = COLS * ROWS
NZ = 8
NB = 8
WIDE = 6 * HALF
OWN_X, OWN_W, OWN_P, FAR_X, FAR_P, FAR_W = range(6)
BLOCK_OF = ((0, 0), (1, 0), (2, 0), (0, 1), (2, 1), (1, 1))
GROUPS = ((0, 3), (3, 2), (5, 1))


def step_kernel(
    edges_total,
    x_hbm, p_hbm, perm_ref, ritz_ref, blocks_ref, adj_ref, link_ref, coef_ref,
    next_ref, gram_ref,
    fx, fp, fw, xlo, xhi, plo, phi, wlo, whi, x_far, p_far, w_far,
    eps, images, part, core_buf, z_buf, z_sum, b_buf, coef_own, scale_out, scale_in,
    load_sem, halo_send, halo_recv, far_send, far_recv,
    core_send, core_recv, z_send, z_recv, b_send, b_recv,
    back_send, back_recv, pair_send, pair_recv, scale_send, scale_recv,
):
    gx, gy, ma = (lax.axis_index(a) for a in ("gx", "gy", "ma"))
    ngx, ngy = lax.axis_size("gx"), lax.axis_size("gy")
    z_id, y_id = lax.rem(gx, NZ), gx // NZ
    core, x_lo = lax.rem(gy, 2), gy // 2
    b_id = y_id * 2 + x_lo
    east, west = {"gx": lax.rem(gx + 1, ngx)}, {"gx": lax.rem(gx + ngx - 1, ngx)}
    north, south = {"gy": lax.rem(gy + 1, ngy)}, {"gy": lax.rem(gy + ngy - 1, ngy)}
    far, pair = {"ma": 1 - ma}, {"gy": gy + 1 - 2 * core}

    def z_peer(step):
        z_to = lax.rem(z_id + step, NZ)
        return z_to, {"gx": y_id * NZ + z_to}

    def b_peer(step):
        b_to = lax.rem(b_id + step, NB)
        return {"gx": (b_to // 2) * NZ + z_id, "gy": lax.rem(b_to, 2) * 2 + core}

    def remote(src, dst, send, recv, device):
        return pltpu.make_async_remote_copy(
            src_ref=src, dst_ref=dst, send_sem=send, recv_sem=recv, device_id=device, device_id_type=MESH
        )

    loads = [
        pltpu.make_async_copy(x_hbm, fx.at[:, pl.ds(1, ROWS)], load_sem.at[0]),
        pltpu.make_async_copy(p_hbm, fp.at[:, pl.ds(1, ROWS)], load_sem.at[1]),
    ]
    for load in loads:
        load.start()

    barrier = pltpu.get_barrier_semaphore()
    for device in (east, west, north, south, far, pair):
        pl.semaphore_signal(barrier, inc=1, device_id=device, device_id_type=MESH)

    @pl.loop(1, NZ)
    def _(step):
        pl.semaphore_signal(barrier, inc=1, device_id=z_peer(step)[1], device_id_type=MESH)

    @pl.loop(1, NB)
    def _(step):
        pl.semaphore_signal(barrier, inc=1, device_id=b_peer(step), device_id_type=MESH)

    pl.semaphore_wait(barrier, 6 + NZ - 1 + NB - 1)
    for load in loads:
        load.wait()

    def halo(k, field, low, high):
        return [
            remote(field.at[1, pl.ds(1, ROWS)], low, halo_send.at[k, 0], halo_recv.at[k, 0], east),
            remote(field.at[0, pl.ds(1, ROWS)], high, halo_send.at[k, 1], halo_recv.at[k, 1], west),
            remote(field.at[:, ROWS], field.at[:, 0], halo_send.at[k, 2], halo_recv.at[k, 2], north),
            remote(field.at[:, 1], field.at[:, ROWS + 1], halo_send.at[k, 3], halo_recv.at[k, 3], south),
        ]

    def zero_rows(field):
        @pl.when(gy == 0)
        def _():
            field[:, 0] = jnp.zeros((COLS, EDGE, HALF), BF16)

        @pl.when(gy == ngy - 1)
        def _():
            field[:, ROWS + 1] = jnp.zeros((COLS, EDGE, HALF), BF16)

    def apply_curl(field, low, high, use):
        for col in range(COLS):
            @pl.loop(0, ROWS)
            def _(row):
                patch = col * ROWS + row
                lower = low[link_ref[0, row]] if col == 0 else field[0, row + 1]
                upper = field[1, row + 1] if col == 0 else high[link_ref[1, row]]
                near = [field[col, row + 1], lower, upper, field[col, row], field[col, row + 2]]
                tiles = [blocks_ref[adj_ref[s, patch]] for s in range(5)]
                image = jnp.dot(
                    jnp.concatenate(tiles, axis=1), jnp.concatenate(near, axis=0), preferred_element_type=F32
                )
                use(col, row, patch, image)

    def gram(refs, first):
        count = len(refs)
        for col in range(COLS):
            @pl.loop(0, 3)
            def _(piece):
                rows = pl.ds(pl.multiple_of(col * ROWS + piece * 4, 4), 4)
                left = [r(col, piece).reshape(4 * EDGE, HALF) for r in refs]
                left = jnp.concatenate(left, axis=1) if count > 1 else left[0]
                right = images[rows].reshape(4 * EDGE, WIDE)
                product = lax.dot_general(
                    left, right, (((0,), (0,)), ((), ())), preferred_element_type=F32
                ).reshape(count, HALF, WIDE)
                if col == 0:
                    @pl.when(piece == 0)
                    def _():
                        part[pl.ds(first, count)] = product

                    @pl.when(piece > 0)
                    def _():
                        part[pl.ds(first, count)] += product
                else:
                    part[pl.ds(first, count)] += product

    def own(field):
        return lambda col, piece: field[col, pl.ds(1 + piece * 4, 4)]

    def other(field):
        return lambda col, piece: field[pl.ds(col * ROWS + piece * 4, 4)]

    half_rows = HALF // 2
    piece_rows = half_rows // NZ
    mine = pl.multiple_of(core * half_rows, half_rows)
    theirs = pl.multiple_of((1 - core) * half_rows, half_rows)

    def reducer(g):
        first, count = GROUPS[g]
        blocks = pl.ds(first, count)

        def core_copy():
            return remote(
                part.at[blocks, pl.ds(theirs, half_rows)], core_buf.at[blocks],
                core_send.at[g], core_recv.at[g], pair,
            )

        def z_copy(step):
            z_to, device = z_peer(step)
            rows = pl.ds(pl.multiple_of(mine + z_to * piece_rows, piece_rows), piece_rows)
            return remote(
                part.at[blocks, rows], z_buf.at[z_id, blocks],
                z_send.at[g, step - 1], z_recv.at[g, step - 1], device,
            )

        def b_copy(step):
            return remote(
                z_sum.at[blocks], b_buf.at[b_id, blocks],
                b_send.at[g, step - 1], b_recv.at[g, step - 1], b_peer(step),
            )

        my_rows = pl.ds(pl.multiple_of(mine + z_id * piece_rows, piece_rows), piece_rows)

        def back_copy(step):
            return remote(
                gram_ref.at[blocks, my_rows], gram_ref.at[blocks, my_rows],
                back_send.at[g, step - 1], back_recv.at[g, step - 1], z_peer(step)[1],
            )

        def pair_copy():
            rows = pl.ds(mine, half_rows)
            return remote(
                gram_ref.at[blocks, rows], gram_ref.at[blocks, rows], pair_send.at[g], pair_recv.at[g], pair
            )

        def each(copy, act):
            @pl.loop(1, NZ)
            def _(step):
                act(copy(step))

        def start_core():
            core_copy().start()

        def start_z():
            core_copy().wait()
            part[blocks, pl.ds(mine, half_rows)] += core_buf[blocks]
            each(z_copy, lambda c: c.start())

        def start_b():
            each(z_copy, lambda c: c.wait())
            total = part[blocks, my_rows]
            for step in range(1, NZ):
                total = total + z_buf[lax.rem(z_id + step, NZ), blocks]
            z_sum[blocks] = total
            b_buf[b_id, blocks] = total
            each(b_copy, lambda c: c.start())

        def start_back():
            each(b_copy, lambda c: c.wait())
            total = b_buf[0, blocks]
            for slot in range(1, NB):
                total = total + b_buf[slot, blocks]
            gram_ref[blocks, my_rows] = total
            each(back_copy, lambda c: c.start())

        def start_pair():
            each(back_copy, lambda c: c.wait())
            pair_copy().start()

        def finish():
            pair_copy().wait()

        return start_core, start_z, start_b, start_back, start_pair, finish

    x_halo = halo(0, fx, xlo, xhi)
    for copy in x_halo:
        copy.start()
    x_cross = [
        remote(fx.at[c, pl.ds(1, ROWS)], x_far.at[pl.ds(c * ROWS, ROWS)], far_send.at[0, c], far_recv.at[0, c], far)
        for c in range(COLS)
    ]
    p_cross = [
        remote(fp.at[c, pl.ds(1, ROWS)], p_far.at[pl.ds(c * ROWS, ROWS)], far_send.at[1, c], far_recv.at[1, c], far)
        for c in range(COLS)
    ]
    w_cross = [
        remote(fw.at[c, pl.ds(1, ROWS)], w_far.at[pl.ds(c * ROWS, ROWS)], far_send.at[2, c], far_recv.at[2, c], far)
        for c in range(COLS)
    ]
    for copy in x_cross + p_cross:
        copy.start()

    @pl.loop(0, PATCHES)
    def _(patch):
        eps[patch] = jnp.broadcast_to(perm_ref[pl.ds(patch, 1)], (EDGE, EDGE)).T

    for copy in x_halo:
        copy.wait()
    p_halo = halo(1, fp, plo, phi)
    for copy in p_halo:
        copy.start()
    zero_rows(fx)

    def use_x(col, row, patch, image):
        values = fx[col, row + 1].astype(F32)
        weight = eps[patch]
        mass = weight * values
        resid = (image - mass * ritz_ref[...]).astype(BF16)
        fw[col, row + 1] = resid
        images[patch, :, pl.ds(0, HALF)] = image.astype(BF16)
        images[patch, :, pl.ds(3 * HALF, HALF)] = mass.astype(BF16)
        images[patch, :, pl.ds(4 * HALF, HALF)] = (weight * resid.astype(F32)).astype(BF16)

    apply_curl(fx, xlo, xhi, use_x)
    w_halo = halo(2, fw, wlo, whi)
    for copy in w_halo:
        copy.start()
    for copy in w_cross:
        copy.start()

    for copy in p_halo:
        copy.wait()
    zero_rows(fp)

    def use_p(col, row, patch, image):
        images[patch, :, pl.ds(2 * HALF, HALF)] = image.astype(BF16)
        images[patch, :, pl.ds(5 * HALF, HALF)] = (eps[patch] * fp[col, row + 1].astype(F32)).astype(BF16)

    apply_curl(fp, plo, phi, use_p)
    for copy in w_halo:
        copy.wait()
    zero_rows(fw)

    def use_w(col, row, patch, image):
        images[patch, :, pl.ds(HALF, HALF)] = image.astype(BF16)

    apply_curl(fw, wlo, whi, use_w)

    first, second, third = reducer(0), reducer(1), reducer(2)
    gram([own(fx), own(fw), own(fp)], 0)
    first[0]()
    for copy in x_cross + p_cross:
        copy.wait()
    first[1]()
    gram([other(x_far), other(p_far)], FAR_X)
    second[0]()
    first[2]()
    second[1]()
    first[3]()
    second[2]()
    first[4]()
    second[3]()
    first[5]()

    row_ids = lax.broadcasted_iota(jnp.int32, (HALF, HALF), 0)
    col_ids = lax.broadcasted_iota(jnp.int32, (HALF, HALF), 1)
    diagonal = row_ids == col_ids
    norms = jnp.where(diagonal, gram_ref[OWN_W, :, pl.ds(4 * HALF, HALF)], 0.0)
    scale_row = lax.rsqrt(jnp.sum(norms, axis=0, keepdims=True) / edges_total + 1e-06)
    scale_col = lax.rsqrt(jnp.sum(norms, axis=1, keepdims=True) / edges_total + 1e-06)
    scale_out[...] = jnp.broadcast_to(scale_row, (8, HALF))
    scale_copy = remote(scale_out, scale_in, scale_send, scale_recv, far)
    scale_copy.start()
    second[4]()
    for copy in w_cross:
        copy.wait()
    gram([other(w_far)], FAR_W)
    third[0]()
    second[5]()
    third[1]()
    scale_copy.wait()
    far_row = jnp.broadcast_to(scale_in[pl.ds(0, 1)], (HALF, HALF))
    far_col = jnp.sum(jnp.where(diagonal, far_row, 0.0), axis=1, keepdims=True)

    cols = pl.ds(pl.multiple_of(ma * HALF, HALF), HALF)
    for k, (block, side) in enumerate(BLOCK_OF):
        half = ma if side == 0 else 1 - ma
        tile = coef_ref[block, pl.ds(pl.multiple_of(half * HALF, HALF), HALF), cols]
        if block == 1:
            tile = (tile.astype(F32) * (scale_col if side == 0 else far_col)).astype(BF16)
        coef_own[pl.ds(k * HALF, HALF)] = tile

    third[2]()
    for col in range(COLS):
        @pl.loop(0, ROWS)
        def _(row):
            patch = col * ROWS + row
            panel = jnp.concatenate(
                [fx[col, row + 1], fw[col, row + 1], fp[col, row + 1], x_far[patch], p_far[patch], w_far[patch]],
                axis=1,
            )
            next_ref[col, row] = jnp.dot(panel, coef_own[...], preferred_element_type=F32).astype(BF16)

    third[3]()
    inverse = 1.0 / edges_total

    def rescale(k):
        block, side = BLOCK_OF[k]
        factor = inverse
        if block == 1:
            factor = (scale_col if side == 0 else far_col) * inverse
        for part_id in range(6):
            cols = pl.ds(part_id * HALF, HALF)
            value = gram_ref[k, :, cols] * factor
            if part_id % 3 == 1:
                value = value * scale_row
            gram_ref[k, :, cols] = value

    for k in range(5):
        rescale(k)
    third[4]()
    third[5]()
    rescale(5)


def on_device(x_modes, p_dirs, permittivity, ritz_values, blocks, adj_types, x_link, coeffs):
    ma = lax.axis_index("ma")
    edges_total = PATCHES * EDGE * lax.axis_size("gx") * lax.axis_size("gy")
    field = pltpu.VMEM((COLS, ROWS + 2, EDGE, HALF), BF16)
    face = pltpu.VMEM((ROWS, EDGE, HALF), BF16)
    whole = pltpu.VMEM((PATCHES, EDGE, HALF), BF16)
    dma = pltpu.SemaphoreType.DMA
    half_rows = HALF // 2
    piece_rows = half_rows // NZ
    vmem = pl.BlockSpec(memory_space=pltpu.VMEM)
    smem = pl.BlockSpec(memory_space=pltpu.SMEM)
    hbm = pl.BlockSpec(memory_space=pl.ANY)
    x_next, gram = pl.pallas_call(
        functools.partial(step_kernel, float(edges_total)),
        out_shape=[
            jax.ShapeDtypeStruct((COLS, ROWS, EDGE, HALF), BF16),
            jax.ShapeDtypeStruct((6, HALF, WIDE), F32),
        ],
        in_specs=[hbm, hbm, vmem, vmem, vmem, smem, smem, vmem],
        out_specs=[vmem, vmem],
        scratch_shapes=[
            field, field, field, face, face, face, face, face, face, whole, whole, whole,
            pltpu.VMEM((PATCHES, EDGE, HALF), F32),
            pltpu.VMEM((PATCHES, EDGE, WIDE), BF16),
            pltpu.VMEM((6, HALF, WIDE), F32),
            pltpu.VMEM((6, half_rows, WIDE), F32),
            pltpu.VMEM((NZ, 6, piece_rows, WIDE), F32),
            pltpu.VMEM((6, piece_rows, WIDE), F32),
            pltpu.VMEM((NB, 6, piece_rows, WIDE), F32),
            pltpu.VMEM((WIDE, HALF), BF16),
            pltpu.VMEM((8, HALF), F32),
            pltpu.VMEM((8, HALF), F32),
            dma((2,)), dma((3, 4)), dma((3, 4)), dma((3, 2)), dma((3, 2)),
            dma((3,)), dma((3,)), dma((3, 7)), dma((3, 7)), dma((3, 7)), dma((3, 7)),
            dma((3, 7)), dma((3, 7)), dma((3,)), dma((3,)), dma, dma,
        ],
        compiler_params=pltpu.CompilerParams(
            collective_id=0, has_side_effects=True, vmem_limit_bytes=56 * 1024 * 1024
        ),
        name="lobpcg_step",
    )(
        x_modes, p_dirs, permittivity.reshape(PATCHES, EDGE), ritz_values.reshape(1, HALF), blocks,
        adj_types.reshape(5, PATCHES), x_link.reshape(2, ROWS), coeffs,
    )
    sides = gram.reshape(2, 3, HALF, WIDE)
    near, away = sides[0], jnp.stack([sides[1, 0], sides[1, 2], sides[1, 1]])
    rows = jnp.where(ma == 0, jnp.concatenate([near, away], axis=1), jnp.concatenate([away, near], axis=1))
    gram_k = rows[:, :, : 3 * HALF].reshape(3, 2 * HALF, 3, HALF)
    gram_m = rows[:, :, 3 * HALF :].reshape(3, 2 * HALF, 3, HALF)
    return x_next, gram_k, gram_m


def solution(mesh):
    placed = (
        P("gx", "gy", None, "ma"),
        P("gx", "gy", None, "ma"),
        P("gx", "gy", None),
        P("ma"),
        P(),
        P(None, "gx", "gy"),
        P(None, "gx", "gy"),
        P(),
    )
    return jax.shard_map(
        on_device,
        mesh=mesh,
        in_specs=placed,
        out_specs=(P("gx", "gy", None, "ma"), P(None, None, None, "ma"), P(None, None, None, "ma")),
        check_vma=False,
    )
```

```python
import functools
import jax
import jax.numpy as jnp
from jax import lax
from jax.experimental import pallas as pl
from jax.experimental.pallas import tpu as pltpu
from jax.sharding import PartitionSpec as P

MESH = pl.DeviceIdType.MESH
F32 = jnp.float32
BF16 = jnp.bfloat16
EDGE = 128
HALF = 128
COLS = 2
ROWS = 12
PATCHES = COLS * ROWS
NZ = 8
NB = 8
KX, MX, MW, MP, KW, KP = range(6)
ROW_OF = ((0, 0), (1, 0), (2, 0), (0, 1), (2, 1), (1, 1))
GROUPS = (((0, 1, 2), (KX, MX, MW, MP)), ((0, 1, 2), (KW, KP)), ((3, 4, 5), (KX, MX, MW, MP, KW, KP)))
SIZES = tuple(len(r) * len(c) for r, c in GROUPS)
STARTS = tuple(sum(SIZES[:g]) for g in range(len(SIZES)))
TILES = sum(SIZES)
NORM_TILE = 1 * 4 + MW


def step_kernel(
    edges_total,
    x_hbm, p_hbm, perm_ref, ritz_ref, blocks_ref, adj_ref, link_ref, coef_ref,
    next_ref, gk_ref, gm_ref,
    fx, fp, fw, fa, xlo, xhi, plo, phi, wlo, whi, alo, ahi, p_far, w_far,
    eps, images, part, core_buf, z_out, z_buf, b_src, b_buf, total_buf, coef_own, scale_out, scale_in, ritz_out, ritz_in,
    load_sem, halo_send, halo_recv, far_send, far_recv,
    core_send, core_recv, z_send, z_recv, b_send, b_recv,
    back_send, back_recv, pair_send, pair_recv, scale_send, scale_recv, ritz_send, ritz_recv,
):
    gx, gy, ma = (lax.axis_index(a) for a in ("gx", "gy", "ma"))
    ngx, ngy = lax.axis_size("gx"), lax.axis_size("gy")
    z_id, y_id = lax.rem(gx, NZ), gx // NZ
    core, x_lo = lax.rem(gy, 2), gy // 2
    b_id = y_id * 2 + x_lo
    east, west = {"gx": lax.rem(gx + 1, ngx)}, {"gx": lax.rem(gx + ngx - 1, ngx)}
    north, south = {"gy": lax.rem(gy + 1, ngy)}, {"gy": lax.rem(gy + ngy - 1, ngy)}
    far, pair = {"ma": 1 - ma}, {"gy": gy + 1 - 2 * core}

    def z_peer(step):
        z_to = lax.rem(z_id + step, NZ)
        return z_to, {"gx": y_id * NZ + z_to}

    def b_peer(step):
        b_to = lax.rem(b_id + step, NB)
        return {"gx": (b_to // 2) * NZ + z_id, "gy": lax.rem(b_to, 2) * 2 + core}

    def remote(src, dst, send, recv, device):
        return pltpu.make_async_remote_copy(
            src_ref=src, dst_ref=dst, send_sem=send, recv_sem=recv, device_id=device, device_id_type=MESH
        )

    def start(copies):
        for copy in copies:
            copy.start()

    def wait(copies):
        for copy in copies:
            copy.wait()

    loads = [
        pltpu.make_async_copy(x_hbm, fx.at[:, pl.ds(1, ROWS)], load_sem.at[0]),
        pltpu.make_async_copy(p_hbm, fp.at[:, pl.ds(1, ROWS)], load_sem.at[1]),
    ]
    start(loads)

    barrier = pltpu.get_barrier_semaphore()
    for device in (east, west, north, south, far, pair):
        pl.semaphore_signal(barrier, inc=1, device_id=device, device_id_type=MESH)

    @pl.loop(1, NZ)
    def _(step):
        pl.semaphore_signal(barrier, inc=1, device_id=z_peer(step)[1], device_id_type=MESH)

    @pl.loop(1, NB)
    def _(step):
        pl.semaphore_signal(barrier, inc=1, device_id=b_peer(step), device_id_type=MESH)

    for col in range(COLS):
        @pl.loop(0, ROWS, unroll=4)
        def _(row):
            eps[col * ROWS + row] = jnp.broadcast_to(perm_ref[row, pl.ds(col, 1)], (EDGE, EDGE)).T

    ritz_out[...] = jnp.broadcast_to(ritz_ref[...], (8, HALF))
    ritz_copy = remote(ritz_out, ritz_in, ritz_send, ritz_recv, far)
    wait(loads)
    pl.semaphore_wait(barrier, 6 + NZ - 1 + NB - 1)

    def halo(k, field, low, high):
        return [
            remote(field.at[0, pl.ds(1, ROWS)], high, halo_send.at[k, 0], halo_recv.at[k, 0], west),
            remote(field.at[1, pl.ds(1, ROWS)], low, halo_send.at[k, 1], halo_recv.at[k, 1], east),
            remote(field.at[:, ROWS], field.at[:, 0], halo_send.at[k, 2], halo_recv.at[k, 2], north),
            remote(field.at[:, 1], field.at[:, ROWS + 1], halo_send.at[k, 3], halo_recv.at[k, 3], south),
        ]

    def zero_rows(field):
        @pl.when(gy == 0)
        def _():
            field[:, 0] = jnp.zeros((COLS, EDGE, HALF), BF16)

        @pl.when(gy == ngy - 1)
        def _():
            field[:, ROWS + 1] = jnp.zeros((COLS, EDGE, HALF), BF16)

    def apply_curl(field, low, high, use, after=None):
        for col in range(COLS):
            @pl.loop(0, ROWS, unroll=4)
            def _(row):
                lower = low[link_ref[0, row]] if col == 0 else field[0, row + 1]
                upper = field[1, row + 1] if col == 0 else high[link_ref[1, row]]
                near = [field[col, row + 1], lower, upper, field[col, row], field[col, row + 2]]
                tiles = [blocks_ref[adj_ref[s, col, row]] for s in range(5)]
                image = jnp.dot(
                    jnp.concatenate(tiles, axis=1), jnp.concatenate(near, axis=0), preferred_element_type=F32
                )
                use(col, row, col * ROWS + row, image)

            if after is not None:
                after(col)

    def column(c):
        return pl.ds(c * HALF, HALF)

    def own(field):
        return lambda col: field[col, pl.ds(1, ROWS)]

    def other(field):
        return lambda col: field[pl.ds(col * ROWS, ROWS)]

    row_refs = (own(fx), own(fw), own(fp), own(fa), other(p_far), other(w_far))

    def gram(g):
        rows, columns = GROUPS[g]
        wide = len(columns) * HALF
        for col in range(COLS):
            left = jnp.concatenate([row_refs[r](col).reshape(ROWS * EDGE, HALF) for r in rows], axis=1)
            right = images[pl.ds(col * ROWS, ROWS), :, pl.ds(columns[0] * HALF, wide)].reshape(ROWS * EDGE, wide)
            product = lax.dot_general(left, right, (((0,), (0,)), ((), ())), preferred_element_type=F32)
            for r in range(len(rows)):
                for c in range(len(columns)):
                    tile = pl.ds((STARTS[g] + r * len(columns) + c) * HALF, HALF)
                    value = product[r * HALF : (r + 1) * HALF, c * HALF : (c + 1) * HALF]
                    part[tile] = value if col == 0 else part[tile] + value

    def reducer(g):
        base, count = STARTS[g] * HALF, SIZES[g]
        half_rows, piece_rows = count * 64, count * 8
        half_base, piece_base = STARTS[g] * 64, STARTS[g] * 8

        def rows_of(offset, size):
            return pl.ds(pl.multiple_of(offset, 16), size)

        mine = rows_of(base + core * half_rows, half_rows)
        theirs = rows_of(base + (1 - core) * half_rows, half_rows)
        my_half = pl.ds(half_base, half_rows)
        my_piece = pl.ds(piece_base, piece_rows)
        piece_total = rows_of(base + core * half_rows + z_id * piece_rows, piece_rows)

        def core_copy():
            return remote(part.at[theirs], core_buf.at[my_half], core_send.at[g], core_recv.at[g], pair)

        def z_copy(step):
            z_to, device = z_peer(step)
            return remote(
                z_out.at[rows_of(half_base + z_to * piece_rows, piece_rows)], z_buf.at[z_id, my_piece],
                z_send.at[g, step - 1], z_recv.at[g, step - 1], device,
            )

        def b_copy(step):
            return remote(
                b_src.at[my_piece], b_buf.at[b_id, my_piece],
                b_send.at[g, step - 1], b_recv.at[g, step - 1], b_peer(step),
            )

        def back_copy(step):
            return remote(
                total_buf.at[piece_total], total_buf.at[piece_total],
                back_send.at[g, step - 1], back_recv.at[g, step - 1], z_peer(step)[1],
            )

        def pair_copy():
            return remote(total_buf.at[mine], total_buf.at[mine], pair_send.at[g], pair_recv.at[g], pair)

        def each(copy, act):
            @pl.loop(1, NZ)
            def _(step):
                act(copy(step))

        def start_core():
            core_copy().start()

        def start_z():
            core_copy().wait()
            z_out[my_half] = (part[mine] + core_buf[my_half]).astype(BF16)
            each(z_copy, lambda c: c.start())

        def start_b():
            total = part[piece_total] + core_buf[rows_of(half_base + z_id * piece_rows, piece_rows)]
            each(z_copy, lambda c: c.wait())
            for step in range(1, NZ):
                total = total + z_buf[lax.rem(z_id + step, NZ), my_piece].astype(F32)
            b_src[my_piece] = total.astype(BF16)
            b_buf[b_id, my_piece] = total.astype(BF16)
            each(b_copy, lambda c: c.start())

        def start_back():
            each(b_copy, lambda c: c.wait())
            total = b_buf[0, my_piece].astype(F32)
            for slot in range(1, NB):
                total = total + b_buf[slot, my_piece].astype(F32)
            total_buf[piece_total] = total.astype(BF16)
            each(back_copy, lambda c: c.start())

        def start_pair():
            each(back_copy, lambda c: c.wait())
            pair_copy().start()

        def finish():
            pair_copy().wait()

        return start_core, start_z, start_b, start_back, start_pair, finish

    first, second, third = reducer(0), reducer(1), reducer(2)

    def cross(k, field, target):
        return [remote(field.at[c, pl.ds(1, ROWS)], target(c), far_send.at[k, c], far_recv.at[k, c], far) for c in range(COLS)]

    x_halo, p_halo, w_halo, a_halo = halo(0, fx, xlo, xhi), halo(1, fp, plo, phi), halo(2, fw, wlo, whi), halo(3, fa, alo, ahi)
    x_cross = cross(0, fx, lambda c: fa.at[c, pl.ds(1, ROWS)])
    p_cross = cross(1, fp, lambda c: p_far.at[pl.ds(c * ROWS, ROWS)])
    start(x_halo)
    start(x_cross)
    ritz_copy.start()

    for col in range(COLS):
        @pl.loop(0, ROWS, unroll=2)
        def _(row):
            patch = col * ROWS + row
            weight = eps[patch]
            images[patch, :, column(MX)] = (weight * fx[col, row + 1].astype(F32)).astype(BF16)
            images[patch, :, column(MP)] = (weight * fp[col, row + 1].astype(F32)).astype(BF16)

    wait(x_halo)
    start(p_halo)
    zero_rows(fx)

    def use_x(col, row, patch, image):
        weight = eps[patch]
        resid = (image - weight * fx[col, row + 1].astype(F32) * ritz_ref[...]).astype(BF16)
        fw[col, row + 1] = resid
        images[patch, :, column(KX)] = image.astype(BF16)
        images[patch, :, column(MW)] = (weight * resid.astype(F32)).astype(BF16)

    apply_curl(fx, xlo, xhi, use_x, lambda col: w_halo[col].start())
    start(w_halo[2:])
    gram(0)
    first[0]()
    wait(x_cross)
    start(a_halo)
    start(p_cross)
    first[1]()
    wait(p_halo)
    zero_rows(fp)

    def use_p(col, row, patch, image):
        images[patch, :, column(KP)] = image.astype(BF16)

    apply_curl(fp, plo, phi, use_p)
    wait(w_halo)
    zero_rows(fw)
    first[2]()

    def use_w(col, row, patch, image):
        images[patch, :, column(KW)] = image.astype(BF16)

    apply_curl(fw, wlo, whi, use_w)
    first[3]()
    gram(1)
    second[0]()
    first[4]()
    wait(a_halo)
    ritz_copy.wait()
    zero_rows(fa)
    second[1]()

    def use_a(col, row, patch, image):
        w_far[patch] = (image - eps[patch] * fa[col, row + 1].astype(F32) * ritz_in[pl.ds(0, 1)]).astype(BF16)

    apply_curl(fa, alo, ahi, use_a)
    first[5]()

    row_ids = lax.broadcasted_iota(jnp.int32, (HALF, HALF), 0)
    col_ids = lax.broadcasted_iota(jnp.int32, (HALF, HALF), 1)
    diagonal = row_ids == col_ids
    norms = jnp.where(diagonal, total_buf[pl.ds(NORM_TILE * HALF, HALF)].astype(F32), 0.0)
    scale_row = lax.rsqrt(jnp.sum(norms, axis=0, keepdims=True) / edges_total + 1e-06)
    scale_col = lax.rsqrt(jnp.sum(norms, axis=1, keepdims=True) / edges_total + 1e-06)
    scale_out[...] = jnp.broadcast_to(scale_row, (8, HALF))
    scale_copy = remote(scale_out, scale_in, scale_send, scale_recv, far)
    scale_copy.start()
    second[2]()
    wait(p_cross)
    gram(2)
    third[0]()
    second[3]()
    scale_copy.wait()
    far_row = jnp.broadcast_to(scale_in[pl.ds(0, 1)], (HALF, HALF))
    far_col = jnp.sum(jnp.where(diagonal, far_row, 0.0), axis=1, keepdims=True)

    cols = pl.ds(pl.multiple_of(ma * HALF, HALF), HALF)
    for k, (block, side) in enumerate(ROW_OF):
        half = ma if side == 0 else 1 - ma
        tile = coef_ref[block, pl.ds(pl.multiple_of(half * HALF, HALF), HALF), cols]
        if block == 1:
            tile = (tile.astype(F32) * (scale_col if side == 0 else far_col)).astype(BF16)
        coef_own[pl.ds(k * HALF, HALF)] = tile

    third[1]()
    second[4]()
    for col in range(COLS):
        @pl.loop(0, ROWS, step=4)
        def _(row):
            panel = jnp.concatenate(
                [f[col, pl.ds(row + 1, 4)] for f in (fx, fw, fp, fa)]
                + [f[pl.ds(col * ROWS + row, 4)] for f in (p_far, w_far)],
                axis=2,
            ).reshape(4 * EDGE, 6 * HALF)
            rotated = jnp.dot(panel, coef_own[...], preferred_element_type=F32)
            next_ref[col, pl.ds(row, 4)] = rotated.astype(BF16).reshape(4, EDGE, HALF)

    third[2]()
    inverse = 1.0 / edges_total

    def rescale(g):
        rows, columns = GROUPS[g]
        for r, row in enumerate(rows):
            block, side = ROW_OF[row]
            factor = inverse
            if block == 1:
                factor = (scale_col if side == 0 else far_col) * inverse
            half = ma if side == 0 else 1 - ma
            place = pl.ds(pl.multiple_of(half * HALF, HALF), HALF)
            for c, col in enumerate(columns):
                tile = STARTS[g] + r * len(columns) + c
                value = total_buf[pl.ds(tile * HALF, HALF)].astype(F32) * factor
                if col in (KW, MW):
                    value = value * scale_row
                out = gk_ref if col in (KX, KW, KP) else gm_ref
                out[block, {KX: 0, MX: 0, KW: 1, MW: 1, KP: 2, MP: 2}[col], place] = value

    rescale(0)
    second[5]()
    rescale(1)
    third[3]()
    third[4]()
    third[5]()
    rescale(2)


def on_device(x_modes, p_dirs, permittivity, ritz_values, blocks, adj_types, x_link, coeffs):
    edges_total = PATCHES * EDGE * lax.axis_size("gx") * lax.axis_size("gy")
    field = pltpu.VMEM((COLS, ROWS + 2, EDGE, HALF), BF16)
    face = pltpu.VMEM((ROWS, EDGE, HALF), BF16)
    whole = pltpu.VMEM((PATCHES, EDGE, HALF), BF16)
    dma = pltpu.SemaphoreType.DMA
    vmem = pl.BlockSpec(memory_space=pltpu.VMEM)
    smem = pl.BlockSpec(memory_space=pltpu.SMEM)
    hbm = pl.BlockSpec(memory_space=pl.ANY)
    lines = TILES * HALF
    x_next, gram_k, gram_m = pl.pallas_call(
        functools.partial(step_kernel, float(edges_total)),
        out_shape=[
            jax.ShapeDtypeStruct((COLS, ROWS, EDGE, HALF), BF16),
            jax.ShapeDtypeStruct((3, 3, 2 * HALF, HALF), F32),
            jax.ShapeDtypeStruct((3, 3, 2 * HALF, HALF), F32),
        ],
        in_specs=[hbm, hbm, vmem, vmem, vmem, smem, smem, vmem],
        out_specs=[vmem, vmem, vmem],
        scratch_shapes=[
            field, field, field, field, face, face, face, face, face, face, face, face, whole, whole,
            pltpu.VMEM((PATCHES, EDGE, HALF), F32),
            pltpu.VMEM((PATCHES, EDGE, 6 * HALF), BF16),
            pltpu.VMEM((lines, HALF), F32),
            pltpu.VMEM((lines // 2, HALF), F32),
            pltpu.VMEM((lines // 2, HALF), BF16),
            pltpu.VMEM((NZ, lines // 16, HALF), BF16),
            pltpu.VMEM((lines // 16, HALF), BF16),
            pltpu.VMEM((NB, lines // 16, HALF), BF16),
            pltpu.VMEM((lines, HALF), BF16),
            pltpu.VMEM((6 * HALF, HALF), BF16),
            pltpu.VMEM((8, HALF), F32),
            pltpu.VMEM((8, HALF), F32),
            pltpu.VMEM((8, HALF), F32),
            pltpu.VMEM((8, HALF), F32),
            dma((2,)), dma((4, 4)), dma((4, 4)), dma((2, 2)), dma((2, 2)),
            dma((3,)), dma((3,)), dma((3, 7)), dma((3, 7)), dma((3, 7)), dma((3, 7)),
            dma((3, 7)), dma((3, 7)), dma((3,)), dma((3,)), dma, dma, dma, dma,
        ],
        compiler_params=pltpu.CompilerParams(
            collective_id=0, has_side_effects=True, vmem_limit_bytes=56 * 1024 * 1024
        ),
        name="lobpcg_step",
    )(
        x_modes, p_dirs, permittivity.transpose(1, 0, 2), ritz_values.reshape(1, HALF), blocks,
        adj_types, x_link.reshape(2, ROWS), coeffs,
    )
    return x_next, gram_k.transpose(0, 2, 1, 3), gram_m.transpose(0, 2, 1, 3)


def solution(mesh):
    placed = (
        P("gx", "gy", None, "ma"),
        P("gx", "gy", None, "ma"),
        P("gx", "gy", None),
        P("ma"),
        P(),
        P(None, "gx", "gy"),
        P(None, "gx", "gy"),
        P(),
    )
    return jax.shard_map(
        on_device,
        mesh=mesh,
        in_specs=placed,
        out_specs=(P("gx", "gy", None, "ma"), P(None, None, None, "ma"), P(None, None, None, "ma")),
        check_vma=False,
    )
```

```python
import functools
import jax
import jax.numpy as jnp
from jax import lax
from jax.experimental import pallas as pl
from jax.experimental.pallas import tpu as pltpu
from jax.sharding import PartitionSpec as P

MESH = pl.DeviceIdType.MESH
F32 = jnp.float32
BF16 = jnp.bfloat16
EDGE = 128
HALF = 128
COLS = 2
ROWS = 12
PATCHES = COLS * ROWS
NZ = 8
NB = 8
KX, MX, MW, MP, KW, KP = range(6)
ROW_OF = ((0, 0), (1, 0), (2, 0), (0, 1), (2, 1), (1, 1))
ALL = (KX, MX, MW, MP, KW, KP)
GROUPS = (((0, 1, 2), ALL), ((3, 4, 5), ALL))
SIZES = tuple(len(r) * len(c) for r, c in GROUPS)
STARTS = tuple(sum(SIZES[:g]) for g in range(len(SIZES)))
TILES = sum(SIZES)
NORM_TILE = len(ALL) + MW


def step_kernel(
    edges_total,
    x_hbm, p_hbm, perm_ref, ritz_ref, blocks_ref, adj_ref, link_ref, coef_ref,
    next_ref, gk_ref, gm_ref,
    fx, fp, fw, fa, xlo, xhi, plo, phi, wlo, whi, alo, ahi, p_far, w_far,
    eps, images, part, core_buf, b_out, b_buf, z_src, z_buf, total_buf, coef_own, scale_out, scale_in, ritz_out, ritz_in,
    load_sem, halo_send, halo_recv, far_send, far_recv,
    core_send, core_recv, b_send, b_recv, z_send, z_recv,
    back_send, back_recv, pair_send, pair_recv, scale_send, scale_recv, ritz_send, ritz_recv,
):
    gx, gy, ma = (lax.axis_index(a) for a in ("gx", "gy", "ma"))
    ngx, ngy = lax.axis_size("gx"), lax.axis_size("gy")
    z_id, y_id = lax.rem(gx, NZ), gx // NZ
    core, x_lo = lax.rem(gy, 2), gy // 2
    b_id = y_id * 2 + x_lo
    east, west = {"gx": lax.rem(gx + 1, ngx)}, {"gx": lax.rem(gx + ngx - 1, ngx)}
    north, south = {"gy": lax.rem(gy + 1, ngy)}, {"gy": lax.rem(gy + ngy - 1, ngy)}
    far, pair = {"ma": 1 - ma}, {"gy": gy + 1 - 2 * core}

    def z_peer(step):
        return {"gx": y_id * NZ + lax.rem(z_id + step, NZ)}

    def b_peer(step):
        b_to = lax.rem(b_id + step, NB)
        return b_to, {"gx": (b_to // 2) * NZ + z_id, "gy": lax.rem(b_to, 2) * 2 + core}

    def remote(src, dst, send, recv, device):
        return pltpu.make_async_remote_copy(
            src_ref=src, dst_ref=dst, send_sem=send, recv_sem=recv, device_id=device, device_id_type=MESH
        )

    def start(copies):
        for copy in copies:
            copy.start()

    def wait(copies):
        for copy in copies:
            copy.wait()

    loads = [
        pltpu.make_async_copy(x_hbm, fx.at[:, pl.ds(1, ROWS)], load_sem.at[0]),
        pltpu.make_async_copy(p_hbm, fp.at[:, pl.ds(1, ROWS)], load_sem.at[1]),
    ]
    start(loads)

    barrier = pltpu.get_barrier_semaphore()
    for device in (east, west, north, south, far, pair):
        pl.semaphore_signal(barrier, inc=1, device_id=device, device_id_type=MESH)

    @pl.loop(1, NZ)
    def _(step):
        pl.semaphore_signal(barrier, inc=1, device_id=z_peer(step), device_id_type=MESH)

    @pl.loop(1, NB)
    def _(step):
        pl.semaphore_signal(barrier, inc=1, device_id=b_peer(step)[1], device_id_type=MESH)

    ritz_out[...] = jnp.broadcast_to(ritz_ref[...], (8, HALF))
    ritz_copy = remote(ritz_out, ritz_in, ritz_send, ritz_recv, far)
    pl.semaphore_wait(barrier, 6 + NZ - 1 + NB - 1)
    wait(loads)

    def halo(k, field, low, high):
        return [
            remote(field.at[0, pl.ds(1, ROWS)], high, halo_send.at[k, 0], halo_recv.at[k, 0], west),
            remote(field.at[1, pl.ds(1, ROWS)], low, halo_send.at[k, 1], halo_recv.at[k, 1], east),
            remote(field.at[:, ROWS], field.at[:, 0], halo_send.at[k, 2], halo_recv.at[k, 2], north),
            remote(field.at[:, 1], field.at[:, ROWS + 1], halo_send.at[k, 3], halo_recv.at[k, 3], south),
        ]

    def zero_rows(field):
        @pl.when(gy == 0)
        def _():
            field[:, 0] = jnp.zeros((COLS, EDGE, HALF), BF16)

        @pl.when(gy == ngy - 1)
        def _():
            field[:, ROWS + 1] = jnp.zeros((COLS, EDGE, HALF), BF16)

    def apply_curl(field, low, high, use, after=None):
        for col in range(COLS):
            @pl.loop(0, ROWS, unroll=4)
            def _(row):
                lower = low[link_ref[0, row]] if col == 0 else field[0, row + 1]
                upper = field[1, row + 1] if col == 0 else high[link_ref[1, row]]
                near = [field[col, row + 1], lower, upper, field[col, row], field[col, row + 2]]
                tiles = [blocks_ref[adj_ref[s, col, row]] for s in range(5)]
                image = jnp.dot(
                    jnp.concatenate(tiles, axis=1), jnp.concatenate(near, axis=0), preferred_element_type=F32
                )
                use(col, row, col * ROWS + row, image)

            if after is not None:
                after(col)

    def column(c):
        return pl.ds(c * HALF, HALF)

    def own(field):
        return lambda col: field[col, pl.ds(1, ROWS)]

    def other(field):
        return lambda col: field[pl.ds(col * ROWS, ROWS)]

    row_refs = (own(fx), own(fw), own(fp), own(fa), other(p_far), other(w_far))

    def gram(g, ready=None):
        rows, columns = GROUPS[g]
        wide = len(columns) * HALF
        for col in range(COLS):
            if ready is not None:
                ready(col)
            left = jnp.concatenate([row_refs[r](col).reshape(ROWS * EDGE, HALF) for r in rows], axis=1)
            right = images[pl.ds(col * ROWS, ROWS), :, pl.ds(columns[0] * HALF, wide)].reshape(ROWS * EDGE, wide)
            product = lax.dot_general(left, right, (((0,), (0,)), ((), ())), preferred_element_type=F32)
            for r in range(len(rows)):
                for c in range(len(columns)):
                    tile = pl.ds((STARTS[g] + r * len(columns) + c) * HALF, HALF)
                    value = product[r * HALF : (r + 1) * HALF, c * HALF : (c + 1) * HALF]
                    part[tile] = value if col == 0 else part[tile] + value

    def reducer(g):
        base, count = STARTS[g] * HALF, SIZES[g]
        half_rows, piece_rows = count * 64, count * 8
        half_base, piece_base = STARTS[g] * 64, STARTS[g] * 8

        def rows_of(offset, size):
            return pl.ds(pl.multiple_of(offset, 16), size)

        mine = rows_of(base + core * half_rows, half_rows)
        theirs = rows_of(base + (1 - core) * half_rows, half_rows)
        my_half = pl.ds(half_base, half_rows)
        my_piece = pl.ds(piece_base, piece_rows)
        piece_total = rows_of(base + core * half_rows + b_id * piece_rows, piece_rows)

        def core_copy():
            return remote(part.at[theirs], core_buf.at[my_half], core_send.at[g], core_recv.at[g], pair)

        def b_copy(step):
            b_to, device = b_peer(step)
            return remote(
                b_out.at[rows_of(half_base + b_to * piece_rows, piece_rows)], b_buf.at[b_id, my_piece],
                b_send.at[g, step - 1], b_recv.at[g, step - 1], device,
            )

        def z_copy(step):
            return remote(
                z_src.at[my_piece], z_buf.at[z_id, my_piece],
                z_send.at[g, step - 1], z_recv.at[g, step - 1], z_peer(step),
            )

        def back_copy(step):
            return remote(
                total_buf.at[piece_total], total_buf.at[piece_total],
                back_send.at[g, step - 1], back_recv.at[g, step - 1], b_peer(step)[1],
            )

        def pair_copy():
            return remote(total_buf.at[mine], total_buf.at[mine], pair_send.at[g], pair_recv.at[g], pair)

        def each(copy, act):
            @pl.loop(1, NZ)
            def _(step):
                act(copy(step))

        def start_core():
            core_copy().start()

        def start_b():
            core_copy().wait()
            b_out[my_half] = (part[mine] + core_buf[my_half]).astype(BF16)
            each(b_copy, lambda c: c.start())

        def start_z():
            total = part[piece_total] + core_buf[rows_of(half_base + b_id * piece_rows, piece_rows)]
            each(b_copy, lambda c: c.wait())
            for step in range(1, NZ):
                total = total + b_buf[lax.rem(b_id + step, NB), my_piece].astype(F32)
            z_src[my_piece] = total.astype(BF16)
            z_buf[z_id, my_piece] = total.astype(BF16)
            each(z_copy, lambda c: c.start())

        def start_zack():
            each(z_copy, lambda c: c.wait())
            total = z_buf[0, my_piece].astype(F32)
            for slot in range(1, NB):
                total = total + z_buf[slot, my_piece].astype(F32)
            total_buf[piece_total] = total.astype(BF16)
            each(back_copy, lambda c: c.start())

        def start_pair():
            each(back_copy, lambda c: c.wait())
            pair_copy().start()

        def finish():
            pair_copy().wait()

        return start_core, start_b, start_z, start_zack, start_pair, finish

    near, away = reducer(0), reducer(1)

    def cross(k, field, target):
        return [remote(field.at[c, pl.ds(1, ROWS)], target(c), far_send.at[k, c], far_recv.at[k, c], far) for c in range(COLS)]

    x_halo, p_halo, w_halo, a_halo = halo(0, fx, xlo, xhi), halo(1, fp, plo, phi), halo(2, fw, wlo, whi), halo(3, fa, alo, ahi)
    x_cross = cross(0, fx, lambda c: fa.at[c, pl.ds(1, ROWS)])
    p_cross = cross(1, fp, lambda c: p_far.at[pl.ds(c * ROWS, ROWS)])
    start(x_halo)
    start(x_cross)
    ritz_copy.start()

    for col in range(COLS):
        @pl.loop(0, ROWS, unroll=4)
        def _(row):
            patch = col * ROWS + row
            weight = jnp.broadcast_to(perm_ref[row, pl.ds(col, 1)], (EDGE, EDGE)).T
            eps[patch] = weight
            images[patch, :, column(MX)] = (weight * fx[col, row + 1].astype(F32)).astype(BF16)
            images[patch, :, column(MP)] = (weight * fp[col, row + 1].astype(F32)).astype(BF16)

    wait(x_halo)
    start(p_halo)
    zero_rows(fx)

    def use_x(col, row, patch, image):
        weight = eps[patch]
        resid = (image - weight * fx[col, row + 1].astype(F32) * ritz_ref[...]).astype(BF16)
        fw[col, row + 1] = resid
        images[patch, :, column(KX)] = image.astype(BF16)
        images[patch, :, column(MW)] = (weight * resid.astype(F32)).astype(BF16)

    apply_curl(fx, xlo, xhi, use_x, lambda col: w_halo[col].start())
    start(w_halo[2:])
    wait(x_cross)
    start(a_halo)
    start(p_cross)
    wait(p_halo)
    zero_rows(fp)

    def use_p(col, row, patch, image):
        images[patch, :, column(KP)] = image.astype(BF16)

    apply_curl(fp, plo, phi, use_p)
    wait(w_halo)
    zero_rows(fw)

    def use_w(col, row, patch, image):
        images[patch, :, column(KW)] = image.astype(BF16)

    apply_curl(fw, wlo, whi, use_w)
    gram(0)
    near[0]()
    wait(a_halo)
    ritz_copy.wait()
    zero_rows(fa)

    def use_a(col, row, patch, image):
        w_far[patch] = (image - eps[patch] * fa[col, row + 1].astype(F32) * ritz_in[pl.ds(0, 1)]).astype(BF16)

    apply_curl(fa, alo, ahi, use_a)
    near[1]()
    wait(p_cross)
    gram(1)
    away[0]()
    near[2]()
    away[1]()
    near[3]()
    away[2]()
    near[4]()
    near[5]()

    row_ids = lax.broadcasted_iota(jnp.int32, (HALF, HALF), 0)
    col_ids = lax.broadcasted_iota(jnp.int32, (HALF, HALF), 1)
    diagonal = row_ids == col_ids
    norms = jnp.where(diagonal, total_buf[pl.ds(NORM_TILE * HALF, HALF)].astype(F32), 0.0)
    scale_row = lax.rsqrt(jnp.sum(norms, axis=0, keepdims=True) / edges_total + 1e-06)
    scale_col = lax.rsqrt(jnp.sum(norms, axis=1, keepdims=True) / edges_total + 1e-06)
    scale_out[...] = jnp.broadcast_to(scale_row, (8, HALF))
    scale_copy = remote(scale_out, scale_in, scale_send, scale_recv, far)
    scale_copy.start()
    away[3]()
    scale_copy.wait()
    far_row = jnp.broadcast_to(scale_in[pl.ds(0, 1)], (HALF, HALF))
    far_col = jnp.sum(jnp.where(diagonal, far_row, 0.0), axis=1, keepdims=True)

    cols = pl.ds(pl.multiple_of(ma * HALF, HALF), HALF)
    for k, (block, side) in enumerate(ROW_OF):
        half = ma if side == 0 else 1 - ma
        tile = coef_ref[block, pl.ds(pl.multiple_of(half * HALF, HALF), HALF), cols]
        if block == 1:
            tile = (tile.astype(F32) * (scale_col if side == 0 else far_col)).astype(BF16)
        coef_own[pl.ds(k * HALF, HALF)] = tile

    for col in range(COLS):
        @pl.loop(0, ROWS, step=4)
        def _(row):
            panel = jnp.concatenate(
                [f[col, pl.ds(row + 1, 4)] for f in (fx, fw, fp, fa)]
                + [f[pl.ds(col * ROWS + row, 4)] for f in (p_far, w_far)],
                axis=2,
            ).reshape(4 * EDGE, 6 * HALF)
            rotated = jnp.dot(panel, coef_own[...], preferred_element_type=F32)
            next_ref[col, pl.ds(row, 4)] = rotated.astype(BF16).reshape(4, EDGE, HALF)

    inverse = 1.0 / edges_total

    def rescale(g):
        rows, columns = GROUPS[g]
        for r, row in enumerate(rows):
            block, side = ROW_OF[row]
            factor = inverse
            if block == 1:
                factor = (scale_col if side == 0 else far_col) * inverse
            half = ma if side == 0 else 1 - ma
            place = pl.ds(pl.multiple_of(half * HALF, HALF), HALF)
            for c, col in enumerate(columns):
                tile = STARTS[g] + r * len(columns) + c
                value = total_buf[pl.ds(tile * HALF, HALF)].astype(F32) * factor
                if col in (KW, MW):
                    value = value * scale_row
                out = gk_ref if col in (KX, KW, KP) else gm_ref
                out[block, {KX: 0, MX: 0, KW: 1, MW: 1, KP: 2, MP: 2}[col], place] = value

    rescale(0)
    away[4]()
    away[5]()
    rescale(1)


def on_device(x_modes, p_dirs, permittivity, ritz_values, blocks, adj_types, x_link, coeffs):
    edges_total = PATCHES * EDGE * lax.axis_size("gx") * lax.axis_size("gy")
    field = pltpu.VMEM((COLS, ROWS + 2, EDGE, HALF), BF16)
    face = pltpu.VMEM((ROWS, EDGE, HALF), BF16)
    whole = pltpu.VMEM((PATCHES, EDGE, HALF), BF16)
    dma = pltpu.SemaphoreType.DMA
    vmem = pl.BlockSpec(memory_space=pltpu.VMEM)
    smem = pl.BlockSpec(memory_space=pltpu.SMEM)
    hbm = pl.BlockSpec(memory_space=pl.ANY)
    lines = TILES * HALF
    x_next, gram_k, gram_m = pl.pallas_call(
        functools.partial(step_kernel, float(edges_total)),
        out_shape=[
            pltpu.VMEM((COLS, ROWS, EDGE, HALF), BF16),
            pltpu.VMEM((3, 3, 2 * HALF, HALF), F32),
            pltpu.VMEM((3, 3, 2 * HALF, HALF), F32),
        ],
        in_specs=[hbm, hbm, vmem, vmem, vmem, smem, smem, vmem],
        out_specs=[vmem, vmem, vmem],
        scratch_shapes=[
            field, field, field, field, face, face, face, face, face, face, face, face, whole, whole,
            pltpu.VMEM((PATCHES, EDGE, HALF), F32),
            pltpu.VMEM((PATCHES, EDGE, 6 * HALF), BF16),
            pltpu.VMEM((lines, HALF), F32),
            pltpu.VMEM((lines // 2, HALF), F32),
            pltpu.VMEM((lines // 2, HALF), BF16),
            pltpu.VMEM((NZ, lines // 16, HALF), BF16),
            pltpu.VMEM((lines // 16, HALF), BF16),
            pltpu.VMEM((NB, lines // 16, HALF), BF16),
            pltpu.VMEM((lines, HALF), BF16),
            pltpu.VMEM((6 * HALF, HALF), BF16),
            pltpu.VMEM((8, HALF), F32),
            pltpu.VMEM((8, HALF), F32),
            pltpu.VMEM((8, HALF), F32),
            pltpu.VMEM((8, HALF), F32),
            dma((2,)), dma((4, 4)), dma((4, 4)), dma((2, 2)), dma((2, 2)),
            dma((2,)), dma((2,)), dma((2, 7)), dma((2, 7)), dma((2, 7)), dma((2, 7)),
            dma((2, 7)), dma((2, 7)), dma((2,)), dma((2,)), dma, dma, dma, dma,
        ],
        compiler_params=pltpu.CompilerParams(
            collective_id=0, has_side_effects=True, vmem_limit_bytes=56 * 1024 * 1024
        ),
        name="lobpcg_step",
    )(
        x_modes, p_dirs, permittivity.transpose(1, 0, 2), ritz_values.reshape(1, HALF), blocks,
        adj_types, x_link.reshape(2, ROWS), coeffs,
    )
    return x_next, gram_k.transpose(0, 2, 1, 3), gram_m.transpose(0, 2, 1, 3)


def solution(mesh):
    placed = (
        P("gx", "gy", None, "ma"),
        P("gx", "gy", None, "ma"),
        P("gx", "gy", None),
        P("ma"),
        P(),
        P(None, "gx", "gy"),
        P(None, "gx", "gy"),
        P(),
    )
    return jax.shard_map(
        on_device,
        mesh=mesh,
        in_specs=placed,
        out_specs=(P("gx", "gy", None, "ma"), P(None, None, None, "ma"), P(None, None, None, "ma")),
        check_vma=False,
    )
```

```python
import functools
import jax
import jax.numpy as jnp
from jax import lax
from jax.experimental import pallas as pl
from jax.experimental.pallas import tpu as pltpu
from jax.sharding import PartitionSpec as P

MESH = pl.DeviceIdType.MESH
F32 = jnp.float32
BF16 = jnp.bfloat16
EDGE = 128
HALF = 128
COLS = 2
ROWS = 12
PATCHES = COLS * ROWS
NZ = 8
NB = 8
KX, MX, MW, MP, KW, KP = range(6)
ROW_OF = ((0, 0), (1, 0), (2, 0), (0, 1), (2, 1), (1, 1))
ALL = (KX, MX, MW, MP, KW, KP)
GROUPS = (((0, 1, 2), ALL), ((3, 4, 5), ALL))
SIZES = tuple(len(r) * len(c) for r, c in GROUPS)
STARTS = tuple(sum(SIZES[:g]) for g in range(len(SIZES)))
TILES = sum(SIZES)
NORM_TILE = len(ALL) + MW


def step_kernel(
    edges_total,
    x_hbm, p_hbm, perm_ref, ritz_ref, blocks_ref, adj_ref, link_ref, coef_ref,
    next_ref, gk_ref, gm_ref,
    fx, fp, fw, fa, xlo, xhi, plo, phi, wlo, whi, alo, ahi, p_far, w_far,
    eps, images, part, core_buf, b_out, b_buf, z_src, z_buf, total_buf, coef_own, scale_out, scale_in, ritz_out, ritz_in,
    load_sem, halo_send, halo_recv, far_send, far_recv,
    core_send, core_recv, b_send, b_recv, z_send, z_recv,
    back_send, back_recv, pair_send, pair_recv, scale_send, scale_recv, ritz_send, ritz_recv,
):
    gx, gy, ma = (lax.axis_index(a) for a in ("gx", "gy", "ma"))
    ngx, ngy = lax.axis_size("gx"), lax.axis_size("gy")
    z_id, y_id = lax.rem(gx, NZ), gx // NZ
    core, x_lo = lax.rem(gy, 2), gy // 2
    b_id = y_id * 2 + x_lo
    east, west = {"gx": lax.rem(gx + 1, ngx)}, {"gx": lax.rem(gx + ngx - 1, ngx)}
    north, south = {"gy": lax.rem(gy + 1, ngy)}, {"gy": lax.rem(gy + ngy - 1, ngy)}
    far, pair = {"ma": 1 - ma}, {"gy": gy + 1 - 2 * core}

    def z_peer(step):
        return {"gx": y_id * NZ + lax.rem(z_id + step, NZ)}

    def b_peer(step):
        b_to = lax.rem(b_id + step, NB)
        return b_to, {"gx": (b_to // 2) * NZ + z_id, "gy": lax.rem(b_to, 2) * 2 + core}

    def remote(src, dst, send, recv, device):
        return pltpu.make_async_remote_copy(
            src_ref=src, dst_ref=dst, send_sem=send, recv_sem=recv, device_id=device, device_id_type=MESH
        )

    def start(copies):
        for copy in copies:
            copy.start()

    def wait(copies):
        for copy in copies:
            copy.wait()

    loads = [
        pltpu.make_async_copy(x_hbm, fx.at[:, pl.ds(1, ROWS)], load_sem.at[0]),
        pltpu.make_async_copy(p_hbm, fp.at[:, pl.ds(1, ROWS)], load_sem.at[1]),
    ]
    start(loads)

    barrier = pltpu.get_barrier_semaphore()
    for device in (east, west, north, south, far, pair):
        pl.semaphore_signal(barrier, inc=1, device_id=device, device_id_type=MESH)

    @pl.loop(1, NZ)
    def _(step):
        pl.semaphore_signal(barrier, inc=1, device_id=z_peer(step), device_id_type=MESH)

    @pl.loop(1, NB)
    def _(step):
        pl.semaphore_signal(barrier, inc=1, device_id=b_peer(step)[1], device_id_type=MESH)

    ritz_out[...] = jnp.broadcast_to(ritz_ref[...], (8, HALF))
    ritz_copy = remote(ritz_out, ritz_in, ritz_send, ritz_recv, far)
    pl.semaphore_wait(barrier, 6 + NZ - 1 + NB - 1)
    wait(loads)

    def halo(k, field, low, high):
        return [
            remote(field.at[0, pl.ds(1, ROWS)], high, halo_send.at[k, 0], halo_recv.at[k, 0], west),
            remote(field.at[1, pl.ds(1, ROWS)], low, halo_send.at[k, 1], halo_recv.at[k, 1], east),
            remote(field.at[:, ROWS], field.at[:, 0], halo_send.at[k, 2], halo_recv.at[k, 2], north),
            remote(field.at[:, 1], field.at[:, ROWS + 1], halo_send.at[k, 3], halo_recv.at[k, 3], south),
        ]

    def zero_rows(field):
        @pl.when(gy == 0)
        def _():
            field[:, 0] = jnp.zeros((COLS, EDGE, HALF), BF16)

        @pl.when(gy == ngy - 1)
        def _():
            field[:, ROWS + 1] = jnp.zeros((COLS, EDGE, HALF), BF16)

    def apply_curl(field, low, high, use, after=None):
        for col in range(COLS):
            @pl.loop(0, ROWS, unroll=4)
            def _(row):
                lower = low[link_ref[0, row]] if col == 0 else field[0, row + 1]
                upper = field[1, row + 1] if col == 0 else high[link_ref[1, row]]
                near = [field[col, row + 1], lower, upper, field[col, row], field[col, row + 2]]
                tiles = [blocks_ref[adj_ref[s, col, row]] for s in range(5)]
                image = jnp.dot(
                    jnp.concatenate(tiles, axis=1), jnp.concatenate(near, axis=0), preferred_element_type=F32
                )
                use(col, row, col * ROWS + row, image)

            if after is not None:
                after(col)

    def column(c):
        return pl.ds(c * HALF, HALF)

    def own(field):
        return lambda col: field[col, pl.ds(1, ROWS)]

    def other(field):
        return lambda col: field[pl.ds(col * ROWS, ROWS)]

    row_refs = (own(fx), own(fw), own(fp), own(fa), other(p_far), other(w_far))

    def gram(g, begin, end, ready=lambda col: None):
        rows, columns = GROUPS[g]
        wide = (end - begin) * HALF
        for col in range(COLS):
            ready(col)
            left = jnp.concatenate([row_refs[r](col).reshape(ROWS * EDGE, HALF) for r in rows], axis=1)
            right = images[pl.ds(col * ROWS, ROWS), :, pl.ds(begin * HALF, wide)].reshape(ROWS * EDGE, wide)
            product = lax.dot_general(left, right, (((0,), (0,)), ((), ())), preferred_element_type=F32)
            for r in range(len(rows)):
                for c in range(begin, end):
                    tile = pl.ds((STARTS[g] + r * len(columns) + c) * HALF, HALF)
                    value = product[r * HALF : (r + 1) * HALF, (c - begin) * HALF : (c - begin + 1) * HALF]
                    part[tile] = value if col == 0 else part[tile] + value

    def reducer(g):
        base, count = STARTS[g] * HALF, SIZES[g]
        half_rows, piece_rows = count * 64, count * 8
        half_base, piece_base = STARTS[g] * 64, STARTS[g] * 8

        def rows_of(offset, size):
            return pl.ds(pl.multiple_of(offset, 16), size)

        mine = rows_of(base + core * half_rows, half_rows)
        theirs = rows_of(base + (1 - core) * half_rows, half_rows)
        my_half = pl.ds(half_base, half_rows)
        my_piece = pl.ds(piece_base, piece_rows)
        piece_total = rows_of(base + core * half_rows + b_id * piece_rows, piece_rows)

        def core_copy():
            return remote(part.at[theirs], core_buf.at[my_half], core_send.at[g], core_recv.at[g], pair)

        def b_copy(step):
            b_to, device = b_peer(step)
            return remote(
                b_out.at[rows_of(half_base + b_to * piece_rows, piece_rows)], b_buf.at[b_id, my_piece],
                b_send.at[g, step - 1], b_recv.at[g, step - 1], device,
            )

        def z_copy(step):
            return remote(
                z_src.at[my_piece], z_buf.at[z_id, my_piece],
                z_send.at[g, step - 1], z_recv.at[g, step - 1], z_peer(step),
            )

        def back_copy(step):
            return remote(
                total_buf.at[piece_total], total_buf.at[piece_total],
                back_send.at[g, step - 1], back_recv.at[g, step - 1], b_peer(step)[1],
            )

        def pair_copy():
            return remote(total_buf.at[mine], total_buf.at[mine], pair_send.at[g], pair_recv.at[g], pair)

        def each(copy, act):
            @pl.loop(1, NZ)
            def _(step):
                act(copy(step))

        def start_core():
            core_copy().start()

        def start_b():
            core_copy().wait()
            b_out[my_half] = (part[mine] + core_buf[my_half]).astype(BF16)
            each(b_copy, lambda c: c.start())

        def start_z():
            total = part[piece_total] + core_buf[rows_of(half_base + b_id * piece_rows, piece_rows)]
            each(b_copy, lambda c: c.wait())
            for step in range(1, NZ):
                total = total + b_buf[lax.rem(b_id + step, NB), my_piece].astype(F32)
            z_src[my_piece] = total.astype(BF16)
            z_buf[z_id, my_piece] = total.astype(BF16)
            each(z_copy, lambda c: c.start())

        def start_zack():
            each(z_copy, lambda c: c.wait())
            total = z_buf[0, my_piece].astype(F32)
            for slot in range(1, NB):
                total = total + z_buf[slot, my_piece].astype(F32)
            total_buf[piece_total] = total.astype(BF16)
            each(back_copy, lambda c: c.start())

        def start_pair():
            each(back_copy, lambda c: c.wait())
            pair_copy().start()

        def finish():
            pair_copy().wait()

        return start_core, start_b, start_z, start_zack, start_pair, finish

    near, away = reducer(0), reducer(1)

    def cross(k, field, target):
        return [remote(field.at[c, pl.ds(1, ROWS)], target(c), far_send.at[k, c], far_recv.at[k, c], far) for c in range(COLS)]

    lead = ROWS - 4

    def faces(k, field, low, high, first, count):
        rows, place = pl.ds(1 + first, count), pl.ds(first, count)
        side = 0 if first == 0 else 4
        return [
            remote(field.at[0, rows], high.at[place], halo_send.at[k, side], halo_recv.at[k, side], west),
            remote(field.at[1, rows], low.at[place], halo_send.at[k, side + 1], halo_recv.at[k, side + 1], east),
        ]

    x_lead, x_rest = faces(0, fx, xlo, xhi, 0, lead), faces(0, fx, xlo, xhi, lead, 4)
    x_halo, p_halo, w_halo, a_halo = halo(0, fx, xlo, xhi)[2:], halo(1, fp, plo, phi), halo(2, fw, wlo, whi), halo(3, fa, alo, ahi)
    x_cross = [
        remote(fx.at[c, pl.ds(1 + r, n)], fa.at[c, pl.ds(1 + r, n)], far_send.at[0, k], far_recv.at[0, k], far)
        for k, (c, r, n) in enumerate(((0, 0, ROWS), (1, 0, ROWS - 4), (1, ROWS - 4, 4)))
    ]
    p_cross = cross(1, fp, lambda c: p_far.at[pl.ds(c * ROWS, ROWS)])
    start(x_lead)
    start(x_rest)
    start(x_halo)
    start(x_cross)
    ritz_copy.start()

    for col in range(COLS):
        @pl.loop(0, ROWS, unroll=4)
        def _(row):
            patch = col * ROWS + row
            weight = jnp.broadcast_to(perm_ref[row, pl.ds(col, 1)], (EDGE, EDGE)).T
            eps[patch] = weight
            images[patch, :, column(MX)] = (weight * fx[col, row + 1].astype(F32)).astype(BF16)
            images[patch, :, column(MP)] = (weight * fp[col, row + 1].astype(F32)).astype(BF16)

    wait(x_lead)
    start(p_halo)
    wait(x_rest)
    wait(x_halo)
    zero_rows(fx)

    def use_x(col, row, patch, image):
        weight = eps[patch]
        resid = (image - weight * fx[col, row + 1].astype(F32) * ritz_ref[...]).astype(BF16)
        fw[col, row + 1] = resid
        images[patch, :, column(KX)] = image.astype(BF16)
        images[patch, :, column(MW)] = (weight * resid.astype(F32)).astype(BF16)

    apply_curl(fx, xlo, xhi, use_x, lambda col: w_halo[col].start())
    start(w_halo[2:])
    gram(0, KX, KW)
    wait(x_cross[:2])
    start(p_cross[:1])
    wait(x_cross[2:])
    start(a_halo)
    start(p_cross[1:])
    wait(p_halo)
    zero_rows(fp)

    def use_p(col, row, patch, image):
        images[patch, :, column(KP)] = image.astype(BF16)

    apply_curl(fp, plo, phi, use_p)
    wait(w_halo)
    zero_rows(fw)

    def use_w(col, row, patch, image):
        images[patch, :, column(KW)] = image.astype(BF16)

    apply_curl(fw, wlo, whi, use_w)
    gram(0, KW, KP + 1)
    near[0]()
    wait(a_halo)
    ritz_copy.wait()
    zero_rows(fa)

    def use_a(col, row, patch, image):
        w_far[patch] = (image - eps[patch] * fa[col, row + 1].astype(F32) * ritz_in[pl.ds(0, 1)]).astype(BF16)

    apply_curl(fa, alo, ahi, use_a)
    near[1]()
    gram(1, KX, KP + 1, lambda col: p_cross[col].wait())
    away[0]()
    near[2]()
    away[1]()
    near[3]()
    away[2]()
    near[4]()
    near[5]()

    row_ids = lax.broadcasted_iota(jnp.int32, (HALF, HALF), 0)
    col_ids = lax.broadcasted_iota(jnp.int32, (HALF, HALF), 1)
    diagonal = row_ids == col_ids
    norms = jnp.where(diagonal, total_buf[pl.ds(NORM_TILE * HALF, HALF)].astype(F32), 0.0)
    scale_row = lax.rsqrt(jnp.sum(norms, axis=0, keepdims=True) / edges_total + 1e-06)
    scale_col = lax.rsqrt(jnp.sum(norms, axis=1, keepdims=True) / edges_total + 1e-06)
    scale_out[...] = jnp.broadcast_to(scale_row, (8, HALF))
    scale_copy = remote(scale_out, scale_in, scale_send, scale_recv, far)
    scale_copy.start()
    away[3]()
    scale_copy.wait()
    far_row = jnp.broadcast_to(scale_in[pl.ds(0, 1)], (HALF, HALF))
    far_col = jnp.sum(jnp.where(diagonal, far_row, 0.0), axis=1, keepdims=True)

    cols = pl.ds(pl.multiple_of(ma * HALF, HALF), HALF)
    for k, (block, side) in enumerate(ROW_OF):
        half = ma if side == 0 else 1 - ma
        tile = coef_ref[block, pl.ds(pl.multiple_of(half * HALF, HALF), HALF), cols]
        if block == 1:
            tile = (tile.astype(F32) * (scale_col if side == 0 else far_col)).astype(BF16)
        coef_own[pl.ds(k * HALF, HALF)] = tile

    for col in range(COLS):
        @pl.loop(0, ROWS, step=4)
        def _(row):
            panel = jnp.concatenate(
                [f[col, pl.ds(row + 1, 4)] for f in (fx, fw, fp, fa)]
                + [f[pl.ds(col * ROWS + row, 4)] for f in (p_far, w_far)],
                axis=2,
            ).reshape(4 * EDGE, 6 * HALF)
            rotated = jnp.dot(panel, coef_own[...], preferred_element_type=F32)
            next_ref[col, pl.ds(row, 4)] = rotated.astype(BF16).reshape(4, EDGE, HALF)

    inverse = 1.0 / edges_total

    def rescale(g):
        rows, columns = GROUPS[g]
        for r, row in enumerate(rows):
            block, side = ROW_OF[row]
            factor = inverse
            if block == 1:
                factor = (scale_col if side == 0 else far_col) * inverse
            half = ma if side == 0 else 1 - ma
            place = pl.ds(pl.multiple_of(half * HALF, HALF), HALF)
            for c, col in enumerate(columns):
                tile = STARTS[g] + r * len(columns) + c
                value = total_buf[pl.ds(tile * HALF, HALF)].astype(F32) * factor
                if col in (KW, MW):
                    value = value * scale_row
                out = gk_ref if col in (KX, KW, KP) else gm_ref
                out[block, {KX: 0, MX: 0, KW: 1, MW: 1, KP: 2, MP: 2}[col], place] = value

    rescale(0)
    away[4]()
    away[5]()
    rescale(1)


def on_device(x_modes, p_dirs, permittivity, ritz_values, blocks, adj_types, x_link, coeffs):
    edges_total = PATCHES * EDGE * lax.axis_size("gx") * lax.axis_size("gy")
    field = pltpu.VMEM((COLS, ROWS + 2, EDGE, HALF), BF16)
    face = pltpu.VMEM((ROWS, EDGE, HALF), BF16)
    whole = pltpu.VMEM((PATCHES, EDGE, HALF), BF16)
    dma = pltpu.SemaphoreType.DMA
    vmem = pl.BlockSpec(memory_space=pltpu.VMEM)
    smem = pl.BlockSpec(memory_space=pltpu.SMEM)
    hbm = pl.BlockSpec(memory_space=pl.ANY)
    lines = TILES * HALF
    x_next, gram_k, gram_m = pl.pallas_call(
        functools.partial(step_kernel, float(edges_total)),
        out_shape=[
            pltpu.VMEM((COLS, ROWS, EDGE, HALF), BF16),
            pltpu.VMEM((3, 3, 2 * HALF, HALF), F32),
            pltpu.VMEM((3, 3, 2 * HALF, HALF), F32),
        ],
        in_specs=[hbm, hbm, vmem, vmem, vmem, smem, smem, vmem],
        out_specs=[vmem, vmem, vmem],
        scratch_shapes=[
            field, field, field, field, face, face, face, face, face, face, face, face, whole, whole,
            pltpu.VMEM((PATCHES, EDGE, HALF), F32),
            pltpu.VMEM((PATCHES, EDGE, 6 * HALF), BF16),
            pltpu.VMEM((lines, HALF), F32),
            pltpu.VMEM((lines // 2, HALF), F32),
            pltpu.VMEM((lines // 2, HALF), BF16),
            pltpu.VMEM((NZ, lines // 16, HALF), BF16),
            pltpu.VMEM((lines // 16, HALF), BF16),
            pltpu.VMEM((NB, lines // 16, HALF), BF16),
            pltpu.VMEM((lines, HALF), BF16),
            pltpu.VMEM((6 * HALF, HALF), BF16),
            pltpu.VMEM((8, HALF), F32),
            pltpu.VMEM((8, HALF), F32),
            pltpu.VMEM((8, HALF), F32),
            pltpu.VMEM((8, HALF), F32),
            dma((2,)), dma((4, 6)), dma((4, 6)), dma((2, 3)), dma((2, 3)),
            dma((2,)), dma((2,)), dma((2, 7)), dma((2, 7)), dma((2, 7)), dma((2, 7)),
            dma((2, 7)), dma((2, 7)), dma((2,)), dma((2,)), dma, dma, dma, dma,
        ],
        compiler_params=pltpu.CompilerParams(
            collective_id=0, has_side_effects=True, vmem_limit_bytes=56 * 1024 * 1024
        ),
        name="lobpcg_step",
    )(
        x_modes, p_dirs, permittivity.transpose(1, 0, 2), ritz_values.reshape(1, HALF), blocks,
        adj_types, x_link.reshape(2, ROWS), coeffs,
    )
    return x_next, gram_k.transpose(0, 2, 1, 3), gram_m.transpose(0, 2, 1, 3)


def solution(mesh):
    placed = (
        P("gx", "gy", None, "ma"),
        P("gx", "gy", None, "ma"),
        P("gx", "gy", None),
        P("ma"),
        P(),
        P(None, "gx", "gy"),
        P(None, "gx", "gy"),
        P(),
    )
    return jax.shard_map(
        on_device,
        mesh=mesh,
        in_specs=placed,
        out_specs=(P("gx", "gy", None, "ma"), P(None, None, None, "ma"), P(None, None, None, "ma")),
        check_vma=False,
    )
```

```python
import functools
import jax
import jax.numpy as jnp
from jax import lax
from jax.experimental import pallas as pl
from jax.experimental.pallas import tpu as pltpu
from jax.sharding import PartitionSpec as P

MESH = pl.DeviceIdType.MESH
F32 = jnp.float32
BF16 = jnp.bfloat16
EDGE = 128
HALF = 128
COLS = 2
ROWS = 12
PATCHES = COLS * ROWS
NZ = 8
NB = 8
KX, MX, MW, MP, KW, KP = range(6)
ROW_OF = ((0, 0), (1, 0), (2, 0), (0, 1), (2, 1), (1, 1))
ALL = (KX, MX, MW, MP, KW, KP)
GROUPS = (((0, 1, 2), ALL), ((3, 4, 5), ALL))
SIZES = tuple(len(r) * len(c) for r, c in GROUPS)
STARTS = tuple(sum(SIZES[:g]) for g in range(len(SIZES)))
TILES = sum(SIZES)
NORM_TILE = len(ALL) + MW


def step_kernel(
    edges_total,
    x_hbm, p_hbm, perm_ref, ritz_ref, blocks_ref, adj_ref, link_ref, coef_ref,
    next_ref, gk_ref, gm_ref,
    fx, fp, fw, fa, xlo, xhi, plo, phi, wlo, whi, alo, ahi, p_far, w_far,
    eps, images, part, core_buf, b_out, b_buf, z_src, z_buf, total_buf, coef_own, scale_out, scale_in, ritz_out, ritz_in,
    load_sem, halo_send, halo_recv, far_send, far_recv,
    core_send, core_recv, b_send, b_recv, z_send, z_recv,
    back_send, back_recv, pair_send, pair_recv, scale_send, scale_recv, ritz_send, ritz_recv,
):
    gx, gy, ma = (lax.axis_index(a) for a in ("gx", "gy", "ma"))
    ngx, ngy = lax.axis_size("gx"), lax.axis_size("gy")
    z_id, y_id = lax.rem(gx, NZ), gx // NZ
    core, x_lo = lax.rem(gy, 2), gy // 2
    b_id = y_id * 2 + x_lo
    east, west = {"gx": lax.rem(gx + 1, ngx)}, {"gx": lax.rem(gx + ngx - 1, ngx)}
    north, south = {"gy": lax.rem(gy + 1, ngy)}, {"gy": lax.rem(gy + ngy - 1, ngy)}
    far, pair = {"ma": 1 - ma}, {"gy": gy + 1 - 2 * core}

    def z_peer(step):
        return {"gx": y_id * NZ + lax.rem(z_id + step, NZ)}

    def b_peer(step):
        b_to = lax.rem(b_id + step, NB)
        return b_to, {"gx": (b_to // 2) * NZ + z_id, "gy": lax.rem(b_to, 2) * 2 + core}

    def remote(src, dst, send, recv, device):
        return pltpu.make_async_remote_copy(
            src_ref=src, dst_ref=dst, send_sem=send, recv_sem=recv, device_id=device, device_id_type=MESH
        )

    def start(copies):
        for copy in copies:
            copy.start()

    def wait(copies):
        for copy in copies:
            copy.wait()

    loads = [
        pltpu.make_async_copy(x_hbm, fx.at[:, pl.ds(1, ROWS)], load_sem.at[0]),
        pltpu.make_async_copy(p_hbm, fp.at[:, pl.ds(1, ROWS)], load_sem.at[1]),
    ]
    start(loads)

    barrier = pltpu.get_barrier_semaphore()
    for device in (east, west, north, south, far, pair):
        pl.semaphore_signal(barrier, inc=1, device_id=device, device_id_type=MESH)

    @pl.loop(1, NZ)
    def _(step):
        pl.semaphore_signal(barrier, inc=1, device_id=z_peer(step), device_id_type=MESH)

    @pl.loop(1, NB)
    def _(step):
        pl.semaphore_signal(barrier, inc=1, device_id=b_peer(step)[1], device_id_type=MESH)

    ritz_out[...] = jnp.broadcast_to(ritz_ref[...], (8, HALF))
    ritz_copy = remote(ritz_out, ritz_in, ritz_send, ritz_recv, far)
    pl.semaphore_wait(barrier, 6 + NZ - 1 + NB - 1)
    wait(loads)

    def halo(k, field, low, high):
        return [
            remote(field.at[0, pl.ds(1, ROWS)], high, halo_send.at[k, 0], halo_recv.at[k, 0], west),
            remote(field.at[1, pl.ds(1, ROWS)], low, halo_send.at[k, 1], halo_recv.at[k, 1], east),
            remote(field.at[:, ROWS], field.at[:, 0], halo_send.at[k, 2], halo_recv.at[k, 2], north),
            remote(field.at[:, 1], field.at[:, ROWS + 1], halo_send.at[k, 3], halo_recv.at[k, 3], south),
        ]

    def zero_rows(field):
        @pl.when(gy == 0)
        def _():
            field[:, 0] = jnp.zeros((COLS, EDGE, HALF), BF16)

        @pl.when(gy == ngy - 1)
        def _():
            field[:, ROWS + 1] = jnp.zeros((COLS, EDGE, HALF), BF16)

    def apply_curl(field, low, high, use, after=None):
        for col in range(COLS):
            @pl.loop(0, ROWS, unroll=4)
            def _(row):
                lower = low[link_ref[0, row]] if col == 0 else field[0, row + 1]
                upper = field[1, row + 1] if col == 0 else high[link_ref[1, row]]
                near = [field[col, row + 1], lower, upper, field[col, row], field[col, row + 2]]
                tiles = [blocks_ref[adj_ref[s, col, row]] for s in range(5)]
                image = jnp.dot(
                    jnp.concatenate(tiles, axis=1), jnp.concatenate(near, axis=0), preferred_element_type=F32
                )
                use(col, row, col * ROWS + row, image)

            if after is not None:
                after(col)

    def column(c):
        return pl.ds(c * HALF, HALF)

    def own(field):
        return lambda col: field[col, pl.ds(1, ROWS)]

    def other(field):
        return lambda col: field[pl.ds(col * ROWS, ROWS)]

    row_refs = (own(fx), own(fw), own(fp), own(fa), other(p_far), other(w_far))

    def gram(g, begin, end, ready=lambda col: None):
        rows, columns = GROUPS[g]
        wide = (end - begin) * HALF
        for col in range(COLS):
            ready(col)
            left = jnp.concatenate([row_refs[r](col).reshape(ROWS * EDGE, HALF) for r in rows], axis=1)
            right = images[pl.ds(col * ROWS, ROWS), :, pl.ds(begin * HALF, wide)].reshape(ROWS * EDGE, wide)
            product = lax.dot_general(left, right, (((0,), (0,)), ((), ())), preferred_element_type=F32)
            for r in range(len(rows)):
                for c in range(begin, end):
                    tile = pl.ds((STARTS[g] + r * len(columns) + c) * HALF, HALF)
                    value = product[r * HALF : (r + 1) * HALF, (c - begin) * HALF : (c - begin + 1) * HALF]
                    part[tile] = value if col == 0 else part[tile] + value

    def reducer(g):
        base, count = STARTS[g] * HALF, SIZES[g]
        half_rows, piece_rows = count * 64, count * 8
        half_base, piece_base = STARTS[g] * 64, STARTS[g] * 8

        def rows_of(offset, size):
            return pl.ds(pl.multiple_of(offset, 16), size)

        mine = rows_of(base + core * half_rows, half_rows)
        theirs = rows_of(base + (1 - core) * half_rows, half_rows)
        my_half = pl.ds(half_base, half_rows)
        my_piece = pl.ds(piece_base, piece_rows)
        piece_total = rows_of(base + core * half_rows + b_id * piece_rows, piece_rows)

        def core_copy():
            return remote(part.at[theirs], core_buf.at[my_half], core_send.at[g], core_recv.at[g], pair)

        def b_copy(step):
            b_to, device = b_peer(step)
            return remote(
                b_out.at[rows_of(half_base + b_to * piece_rows, piece_rows)], b_buf.at[b_id, my_piece],
                b_send.at[g, step - 1], b_recv.at[g, step - 1], device,
            )

        def z_copy(step):
            return remote(
                z_src.at[my_piece], z_buf.at[z_id, my_piece],
                z_send.at[g, step - 1], z_recv.at[g, step - 1], z_peer(step),
            )

        def back_copy(step):
            return remote(
                total_buf.at[piece_total], total_buf.at[piece_total],
                back_send.at[g, step - 1], back_recv.at[g, step - 1], b_peer(step)[1],
            )

        def pair_copy():
            return remote(total_buf.at[mine], total_buf.at[mine], pair_send.at[g], pair_recv.at[g], pair)

        def each(copy, act):
            @pl.loop(1, NZ)
            def _(step):
                act(copy(step))

        def start_core():
            core_copy().start()

        def start_b():
            core_copy().wait()
            b_out[my_half] = (part[mine] + core_buf[my_half]).astype(BF16)
            each(b_copy, lambda c: c.start())

        def start_z():
            total = part[piece_total] + core_buf[rows_of(half_base + b_id * piece_rows, piece_rows)]
            each(b_copy, lambda c: c.wait())
            for step in range(1, NZ):
                total = total + b_buf[lax.rem(b_id + step, NB), my_piece].astype(F32)
            z_src[my_piece] = total.astype(BF16)
            z_buf[z_id, my_piece] = total.astype(BF16)
            each(z_copy, lambda c: c.start())

        def start_zack():
            each(z_copy, lambda c: c.wait())
            total = z_buf[0, my_piece].astype(F32)
            for slot in range(1, NB):
                total = total + z_buf[slot, my_piece].astype(F32)
            total_buf[piece_total] = total.astype(BF16)
            each(back_copy, lambda c: c.start())

        def start_pair():
            each(back_copy, lambda c: c.wait())
            pair_copy().start()

        def finish():
            pair_copy().wait()

        return start_core, start_b, start_z, start_zack, start_pair, finish

    near, away = reducer(0), reducer(1)

    def cross(k, field, target):
        return [remote(field.at[c, pl.ds(1, ROWS)], target(c), far_send.at[k, c], far_recv.at[k, c], far) for c in range(COLS)]

    lead = ROWS - 4

    def faces(k, field, low, high, first, count):
        rows, place = pl.ds(1 + first, count), pl.ds(first, count)
        side = 0 if first == 0 else 4
        return [
            remote(field.at[0, rows], high.at[place], halo_send.at[k, side], halo_recv.at[k, side], west),
            remote(field.at[1, rows], low.at[place], halo_send.at[k, side + 1], halo_recv.at[k, side + 1], east),
        ]

    x_lead, x_rest = faces(0, fx, xlo, xhi, 0, lead), faces(0, fx, xlo, xhi, lead, 4)
    x_halo, p_halo, w_halo, a_halo = halo(0, fx, xlo, xhi)[2:], halo(1, fp, plo, phi), halo(2, fw, wlo, whi), halo(3, fa, alo, ahi)
    x_cross = [
        remote(fx.at[c, pl.ds(1 + r, n)], fa.at[c, pl.ds(1 + r, n)], far_send.at[0, k], far_recv.at[0, k], far)
        for k, (c, r, n) in enumerate(((0, 0, ROWS), (1, 0, ROWS - 4), (1, ROWS - 4, 4)))
    ]
    p_cross = cross(1, fp, lambda c: p_far.at[pl.ds(c * ROWS, ROWS)])
    start(x_lead)
    start(x_rest)
    start(x_halo)
    start(x_cross)
    ritz_copy.start()

    for col in range(COLS):
        @pl.loop(0, ROWS, unroll=4)
        def _(row):
            patch = col * ROWS + row
            weight = jnp.broadcast_to(perm_ref[row, pl.ds(col, 1)], (EDGE, EDGE)).T
            eps[patch] = weight
            images[patch, :, column(MX)] = (weight * fx[col, row + 1].astype(F32)).astype(BF16)
            images[patch, :, column(MP)] = (weight * fp[col, row + 1].astype(F32)).astype(BF16)

    wait(x_lead)
    start(p_halo)
    wait(x_rest)
    wait(x_halo)
    zero_rows(fx)

    def use_x(col, row, patch, image):
        weight = eps[patch]
        resid = (image - weight * fx[col, row + 1].astype(F32) * ritz_ref[...]).astype(BF16)
        fw[col, row + 1] = resid
        images[patch, :, column(KX)] = image.astype(BF16)
        images[patch, :, column(MW)] = (weight * resid.astype(F32)).astype(BF16)

    apply_curl(fx, xlo, xhi, use_x, lambda col: w_halo[col].start())
    start(w_halo[2:])
    gram(0, KX, KW)
    wait(x_cross[:2])
    start(p_cross[:1])
    wait(x_cross[2:])
    start(a_halo)
    start(p_cross[1:])
    wait(p_halo)
    zero_rows(fp)

    def use_p(col, row, patch, image):
        images[patch, :, column(KP)] = image.astype(BF16)

    apply_curl(fp, plo, phi, use_p)
    wait(w_halo)
    zero_rows(fw)

    def use_w(col, row, patch, image):
        images[patch, :, column(KW)] = image.astype(BF16)

    apply_curl(fw, wlo, whi, use_w)
    gram(0, KW, KP + 1)
    near[0]()
    wait(a_halo)
    ritz_copy.wait()
    zero_rows(fa)

    def use_a(col, row, patch, image):
        w_far[patch] = (image - eps[patch] * fa[col, row + 1].astype(F32) * ritz_in[pl.ds(0, 1)]).astype(BF16)

    apply_curl(fa, alo, ahi, use_a)
    near[1]()
    gram(1, KX, KP + 1, lambda col: p_cross[col].wait())
    away[0]()
    near[2]()
    away[1]()
    near[3]()
    away[2]()
    near[4]()
    near[5]()

    row_ids = lax.broadcasted_iota(jnp.int32, (HALF, HALF), 0)
    col_ids = lax.broadcasted_iota(jnp.int32, (HALF, HALF), 1)
    diagonal = row_ids == col_ids
    norms = jnp.where(diagonal, total_buf[pl.ds(NORM_TILE * HALF, HALF)].astype(F32), 0.0)
    scale_row = lax.rsqrt(jnp.sum(norms, axis=0, keepdims=True) / edges_total + 1e-06)
    scale_col = lax.rsqrt(jnp.sum(norms, axis=1, keepdims=True) / edges_total + 1e-06)
    scale_out[...] = jnp.broadcast_to(scale_row, (8, HALF))
    scale_copy = remote(scale_out, scale_in, scale_send, scale_recv, far)
    scale_copy.start()
    away[3]()
    scale_copy.wait()
    far_row = jnp.broadcast_to(scale_in[pl.ds(0, 1)], (HALF, HALF))
    far_col = jnp.sum(jnp.where(diagonal, far_row, 0.0), axis=1, keepdims=True)

    cols = pl.ds(pl.multiple_of(ma * HALF, HALF), HALF)
    for k, (block, side) in enumerate(ROW_OF):
        half = ma if side == 0 else 1 - ma
        tile = coef_ref[block, pl.ds(pl.multiple_of(half * HALF, HALF), HALF), cols]
        if block == 1:
            tile = (tile.astype(F32) * (scale_col if side == 0 else far_col)).astype(BF16)
        coef_own[pl.ds(k * HALF, HALF)] = tile

    for col in range(COLS):
        @pl.loop(0, ROWS, step=4)
        def _(row):
            panel = jnp.concatenate(
                [f[col, pl.ds(row + 1, 4)] for f in (fx, fw, fp, fa)]
                + [f[pl.ds(col * ROWS + row, 4)] for f in (p_far, w_far)],
                axis=2,
            ).reshape(4 * EDGE, 6 * HALF)
            rotated = jnp.dot(panel, coef_own[...], preferred_element_type=F32)
            next_ref[col, pl.ds(row, 4)] = rotated.astype(BF16).reshape(4, EDGE, HALF)

    inverse = 1.0 / edges_total

    def rescale(g, begin, end):
        rows, columns = GROUPS[g]
        for r, row in enumerate(rows):
            block, side = ROW_OF[row]
            factor = inverse
            if block == 1:
                factor = (scale_col if side == 0 else far_col) * inverse
            half = ma if side == 0 else 1 - ma
            place = pl.ds(pl.multiple_of(half * HALF, HALF), HALF)
            for c, col in enumerate(columns):
                if not begin <= r * len(columns) + c < end:
                    continue
                tile = STARTS[g] + r * len(columns) + c
                value = total_buf[pl.ds(tile * HALF, HALF)].astype(F32) * factor
                if col in (KW, MW):
                    value = value * scale_row
                out = gk_ref if col in (KX, KW, KP) else gm_ref
                out[block, {KX: 0, MX: 0, KW: 1, MW: 1, KP: 2, MP: 2}[col], place] = value

    rescale(0, 0, SIZES[0])
    away[4]()
    middle = SIZES[1] // 2

    @pl.when(core == 0)
    def _():
        rescale(1, 0, middle)

    @pl.when(core == 1)
    def _():
        rescale(1, middle, SIZES[1])

    away[5]()

    @pl.when(core == 0)
    def _():
        rescale(1, middle, SIZES[1])

    @pl.when(core == 1)
    def _():
        rescale(1, 0, middle)


def on_device(x_modes, p_dirs, permittivity, ritz_values, blocks, adj_types, x_link, coeffs):
    edges_total = PATCHES * EDGE * lax.axis_size("gx") * lax.axis_size("gy")
    field = pltpu.VMEM((COLS, ROWS + 2, EDGE, HALF), BF16)
    face = pltpu.VMEM((ROWS, EDGE, HALF), BF16)
    whole = pltpu.VMEM((PATCHES, EDGE, HALF), BF16)
    dma = pltpu.SemaphoreType.DMA
    vmem = pl.BlockSpec(memory_space=pltpu.VMEM)
    smem = pl.BlockSpec(memory_space=pltpu.SMEM)
    hbm = pl.BlockSpec(memory_space=pl.ANY)
    lines = TILES * HALF
    x_next, gram_k, gram_m = pl.pallas_call(
        functools.partial(step_kernel, float(edges_total)),
        out_shape=[
            pltpu.VMEM((COLS, ROWS, EDGE, HALF), BF16),
            pltpu.VMEM((3, 3, 2 * HALF, HALF), F32),
            pltpu.VMEM((3, 3, 2 * HALF, HALF), F32),
        ],
        in_specs=[hbm, hbm, vmem, vmem, vmem, smem, smem, vmem],
        out_specs=[vmem, vmem, vmem],
        scratch_shapes=[
            field, field, field, field, face, face, face, face, face, face, face, face, whole, whole,
            pltpu.VMEM((PATCHES, EDGE, HALF), F32),
            pltpu.VMEM((PATCHES, EDGE, 6 * HALF), BF16),
            pltpu.VMEM((lines, HALF), F32),
            pltpu.VMEM((lines // 2, HALF), F32),
            pltpu.VMEM((lines // 2, HALF), BF16),
            pltpu.VMEM((NZ, lines // 16, HALF), BF16),
            pltpu.VMEM((lines // 16, HALF), BF16),
            pltpu.VMEM((NB, lines // 16, HALF), BF16),
            pltpu.VMEM((lines, HALF), BF16),
            pltpu.VMEM((6 * HALF, HALF), BF16),
            pltpu.VMEM((8, HALF), F32),
            pltpu.VMEM((8, HALF), F32),
            pltpu.VMEM((8, HALF), F32),
            pltpu.VMEM((8, HALF), F32),
            dma((2,)), dma((4, 6)), dma((4, 6)), dma((2, 3)), dma((2, 3)),
            dma((2,)), dma((2,)), dma((2, 7)), dma((2, 7)), dma((2, 7)), dma((2, 7)),
            dma((2, 7)), dma((2, 7)), dma((2,)), dma((2,)), dma, dma, dma, dma,
        ],
        compiler_params=pltpu.CompilerParams(
            collective_id=0, has_side_effects=True, vmem_limit_bytes=56 * 1024 * 1024
        ),
        name="lobpcg_step",
    )(
        x_modes, p_dirs, permittivity.transpose(1, 0, 2), ritz_values.reshape(1, HALF), blocks,
        adj_types, x_link.reshape(2, ROWS), coeffs,
    )
    return x_next, gram_k.transpose(0, 2, 1, 3), gram_m.transpose(0, 2, 1, 3)


def solution(mesh):
    placed = (
        P("gx", "gy", None, "ma"),
        P("gx", "gy", None, "ma"),
        P("gx", "gy", None),
        P("ma"),
        P(),
        P(None, "gx", "gy"),
        P(None, "gx", "gy"),
        P(),
    )
    return jax.shard_map(
        on_device,
        mesh=mesh,
        in_specs=placed,
        out_specs=(P("gx", "gy", None, "ma"), P(None, None, None, "ma"), P(None, None, None, "ma")),
        check_vma=False,
    )
```
